128 devices in a mesh: dp: 8 (over y_hi, x), seq: 16 (over y_lo, z, core).
Axes of the slice: x: 4, y: 4 (y_hi: 2, y_lo: 2; y = y_hi * 2 + y_lo), z: 4, core: 2. Of those that a mesh axis runs over, the one named last changes fastest.
Arguments:
- tokens: bfloat16 [16384, 2048], P(('dp', 'seq')), may hold values from -6 to 6
- doc_lengths: int32 [8, 3], P('dp'), may hold values from 32 to 2048, as said below
- first_gain: bfloat16 [2048], P('seq'), may hold values from 0.25 to 1.75
- query_down: bfloat16 [2048, 1024], P('seq'), may hold values from -0.125 to 0.125
- key_proj: bfloat16 [2048, 256], P('seq'), may hold values from -0.125 to 0.125
- value_proj: bfloat16 [2048, 256], P('seq'), may hold values from -0.125 to 0.125
- query_gain: bfloat16 [1024], P('seq'), may hold values from 0.25 to 1.75
- query_up: bfloat16 [1024, 4096], P('seq'), may hold values from -0.1875 to 0.1875
- out_proj: bfloat16 [4096, 2048], P('seq'), may hold values from -0.75 to 0.75
- second_gain: bfloat16 [2048], P('seq'), may hold values from 0.25 to 1.75
- gate_proj: bfloat16 [2048, 5632], P('seq'), may hold values from -0.125 to 0.125
- up_proj: bfloat16 [2048, 5632], P('seq'), may hold values from -0.125 to 0.125
- down_proj: bfloat16 [5632, 2048], P('seq'), may hold values from -0.078125 to 0.078125
- cotangent: bfloat16 [16384, 2048], P(('dp', 'seq')), may hold values from -6 to 6
Outputs:
- layer_out: bfloat16 [16384, 2048], P(('dp', 'seq'))
- input_grad: float32 [16384, 2048], P(('dp', 'seq'))
- first_gain_grad: float32 [2048], P('seq')
- query_down_grad: float32 [2048, 1024], P('seq')
- key_proj_grad: float32 [2048, 256], P('seq')
- value_proj_grad: float32 [2048, 256], P('seq')
- query_gain_grad: float32 [1024], P('seq')
- query_up_grad: float32 [1024, 4096], P('seq')
- out_proj_grad: float32 [4096, 2048], P('seq')
- second_gain_grad: float32 [2048], P('seq')
- gate_proj_grad: float32 [2048, 5632], P('seq')
- up_proj_grad: float32 [2048, 5632], P('seq')
- down_proj_grad: float32 [5632, 2048], P('seq')
The draws below stay inside these ranges and needn't reach their ends.
Inputs may be any that keep to these rules, and one draw needn't show every extreme that they name: Each row of doc_lengths sums to 2048. In each row one document, in a slot drawn from the seed, holds at least 1922 tokens; the others hold 32 to 63 each.
All inputs are finite; a program needn't handle non-finite values.
Results may differ from the reference program's by a relative error of at most 0.028.
Values may be sent and summed in bfloat16 or wider, within the bound.
No kernel may reach another device: no remote copies, remote signals or barrier semaphores. Data moves between devices by JAX's collectives and lax.ppermute only.
A program may use at most 320 MiB of HBM per device.

```python
import jax
import jax.numpy as jnp
from jax import lax

D = 2048
Q_LATENT = 1024
HEADS = 16
HEAD_DIM = 256
FF = 5632
TOK_DEV = 128
DOCS = 3
TOKENS = 16384
N_DP = 8
N_SEQ = 16


def draw_doc_lengths(key, part):
    key = jax.random.fold_in(key, 11)
    key_pick, key_length = jax.random.split(key)
    longest = jax.random.randint(key_pick, (N_DP, 1), 0, DOCS)
    raw_draw = jax.random.randint(key_length, (N_DP, DOCS), 0, 16)
    short_least = TOK_DEV // 4
    short_most = TOK_DEV // 2 - 1
    shorts = short_least + raw_draw * raw_draw * raw_draw * (short_most - short_least) // 3375
    slots = jnp.arange(DOCS, dtype=jnp.int32)[None, :]
    is_long = slots == longest
    shorts = jnp.where(is_long, 0, shorts)
    long_length = TOK_DEV * N_SEQ - jnp.sum(shorts, axis=1, keepdims=True)
    return jnp.where(is_long, long_length, shorts).astype(jnp.int32)


def levels(rng, shape, shards, least, high):
    def one(axis_at, parts):
        draws = jax.random.uniform(jax.random.fold_in(jax.random.fold_in(rng, 6), axis_at), (parts,), jnp.float32, least / len(shards), high / len(shards))
        return jnp.repeat(jnp.exp(draws), shape[axis_at] // parts).reshape((-1,) + (1,) * (len(shape) - axis_at - 1))

    factor_of = one(*shards[0])
    for cut in shards[1:]:
        factor_of = factor_of * one(*cut)
    return factor_of


def centred(stream_key, dims, width, bound, shards=(), kind=jnp.bfloat16):
    result = jax.random.normal(stream_key, dims, jnp.float32) * width
    if len(shards) > 0:
        result = levels(stream_key, dims, shards, -0.22, 0.18) * result
    return jnp.clip(result, min=-bound, max=bound).astype(kind)


def setup_inputs(seed: int = 0) -> dict:
    streams_of = jax.random.split(jax.random.key(seed), 15)
    return {
        "tokens": centred(streams_of[0], (TOKENS, D), 1.0, 6.0, ((0, 128),)),
        "doc_lengths": draw_doc_lengths(jax.random.fold_in(streams_of[14], 71), 0),
        "first_gain": jnp.clip(1.0 + 0.15 * jax.random.normal(streams_of[2], (D,), jnp.float32), 0.25, 1.75).astype(jnp.bfloat16),
        "query_down": centred(streams_of[3], (D, Q_LATENT), D ** -0.5, 0.125, ((0, 16),)),
        "key_proj": centred(streams_of[4], (D, HEAD_DIM), D ** -0.5, 0.125, ((0, 16),)),
        "value_proj": centred(streams_of[5], (D, HEAD_DIM), D ** -0.5, 0.125, ((0, 16),)),
        "query_gain": jnp.clip(1.0 + 0.15 * jax.random.normal(streams_of[6], (Q_LATENT,), jnp.float32), 0.25, 1.75).astype(jnp.bfloat16),
        "query_up": centred(streams_of[7], (Q_LATENT, HEADS * HEAD_DIM), Q_LATENT ** -0.5, 0.1875, ((0, 16),)),
        "out_proj": centred(streams_of[8], (HEADS * HEAD_DIM, D), (max(HEADS * HEAD_DIM // 64, 2)) ** -0.5, 0.75, ((0, 16),)),
        "second_gain": jnp.clip(1.0 + 0.15 * jax.random.normal(streams_of[9], (D,), jnp.float32), 0.25, 1.75).astype(jnp.bfloat16),
        "gate_proj": centred(streams_of[10], (D, FF), D ** -0.5, 0.125, ((0, 16),)),
        "up_proj": centred(streams_of[11], (D, FF), D ** -0.5, 0.125, ((0, 16),)),
        "down_proj": centred(streams_of[12], (FF, D), FF ** -0.5, 0.078125, ((0, 16),)),
        "cotangent": centred(streams_of[13], (TOKENS, D), 1.0, 6.0, ((0, 128),)),
    }


HIGH = lax.Precision.HIGHEST
NORM_EPSILON = 1e-05

@jax.custom_vjp
def low(v):
    return lax.optimization_barrier(v.astype(jnp.bfloat16)).astype(jnp.float32)

@jax.custom_vjp
def low_back(v):
    return v

def low_keep(v):
    return (low(v), None)

def low_pass(kept, grad):
    return (grad,)

def back_keep(v):
    return (v, None)

def back_low(kept, grad):
    return (low(grad),)
low.defvjp(low_keep, low_pass)
low_back.defvjp(back_keep, back_low)

def matmul(left, right):
    return jnp.dot(left, right, precision=HIGH)

def rms_norm(values, gain_row):
    return values * lax.rsqrt(lax.optimization_barrier(jnp.mean(values * values, axis=-1, keepdims=True)) + NORM_EPSILON) * gain_row

def layout(lengths, token_index):
    doc_ends = jnp.cumsum(lengths).astype(jnp.int32)
    starts = (doc_ends - lengths).astype(jnp.int32)
    doc_id = lax.optimization_barrier(jnp.sum((token_index[:, None] >= doc_ends[None, :]).astype(jnp.int32), axis=1)).astype(jnp.int32)
    numbers = jnp.arange(lengths.shape[0], dtype=jnp.int32)
    doc_start = lax.optimization_barrier(jnp.sum(jnp.where(doc_id[:, None] == numbers[None, :], starts[None, :], 0), axis=1)).astype(jnp.int32)
    return (doc_id, token_index - doc_start)

def rope_tables(position, head_width):
    half_width = head_width // 2
    frequency = 10000.0 ** (-(2.0 * jnp.arange(half_width, dtype=jnp.float32)) / head_width)
    angles = position.astype(jnp.float32)[:, None] * frequency[None, :]
    cosine = jnp.cos(angles)
    sine_table = jnp.sin(angles)
    return (jnp.concatenate([cosine, cosine], axis=-1), jnp.concatenate([sine_table, sine_table], axis=-1))

def rotate(values, cosine, sine_table):
    half_width = values.shape[-1] // 2
    turned = jnp.concatenate([-values[..., half_width:], values[..., :half_width]], axis=-1)
    return values * cosine + turned * sine_table

def group_forward(params, group_tokens, lengths):
    first_gain, query_down, key_proj, value_proj, query_gain, query_up, out_proj, second_gain, gate_proj, up_proj, down_proj = params
    group_size = group_tokens.shape[0]
    token_index = jnp.arange(group_size, dtype=jnp.int32)
    doc_id, position = layout(lengths, token_index)
    cosine, sine_table = rope_tables(position, HEAD_DIM)
    normed = low(rms_norm(group_tokens, first_gain))
    latent = low_back(matmul(normed, query_down))
    latent_n = low(rms_norm(latent, query_gain))
    queries = low_back(matmul(latent_n, query_up)).reshape(group_size, HEADS, HEAD_DIM)
    key_raw = low_back(matmul(normed, key_proj))
    value_raw = low_back(matmul(normed, value_proj))
    query_rot = low(rotate(queries, cosine[:, None, :], sine_table[:, None, :]))
    key_rot = low(rotate(key_raw, cosine, sine_table))
    value_low = low(value_raw)
    block_rows = min(512, group_size)
    score_scale = HEAD_DIM ** (-0.5)

    def attend(pieces):
        query_block, doc_block, index_block = pieces
        scores = low_back(jnp.einsum('qhd,kd->hqk', query_block, key_rot, precision=HIGH)) * score_scale
        allowed = (doc_block[:, None] == doc_id[None, :]) & (token_index[None, :] <= index_block[:, None])
        scores = jnp.where(allowed[None], scores, -1e+30)
        shifted = scores - lax.optimization_barrier(jnp.max(scores, axis=-1, keepdims=True))
        exponent = jnp.exp(shifted)
        totals = lax.optimization_barrier(jnp.sum(exponent, axis=-1, keepdims=True))
        mixed = jnp.einsum('hqk,kd->qhd', low(exponent), value_low, precision=HIGH)
        return low_back(mixed / jnp.transpose(totals, (1, 0, 2)))
    blocks = group_size // block_rows
    attended = lax.map(jax.checkpoint(attend), (query_rot.reshape(blocks, block_rows, HEADS, HEAD_DIM), doc_id.reshape(blocks, block_rows), token_index.reshape(blocks, block_rows)))
    attended = low(attended.reshape(group_size, HEADS * HEAD_DIM))
    residual = group_tokens + low_back(matmul(attended, out_proj))
    normed_two = low(rms_norm(residual, second_gain))
    gate_values = low_back(matmul(normed_two, gate_proj))
    up_values = low_back(matmul(normed_two, up_proj))
    hidden = low(gate_values * jax.nn.sigmoid(gate_values) * up_values)
    return residual + low_back(matmul(hidden, down_proj))

def reference(tokens, doc_lengths, first_gain, query_down, key_proj, value_proj, query_gain, query_up, out_proj, second_gain, gate_proj, up_proj, down_proj, cotangent):
    params = tuple((weight.astype(jnp.float32) for weight in (first_gain, query_down, key_proj, value_proj, query_gain, query_up, out_proj, second_gain, gate_proj, up_proj, down_proj)))
    tokens_float = tokens.astype(jnp.float32)

    def forward(tokens_in, params_in):

        def one_group(pieces):
            return jax.checkpoint(group_forward)(params_in, pieces[0], pieces[1])
        outputs = lax.map(one_group, (tokens_in.reshape(N_DP, -1, D), doc_lengths))
        return outputs.reshape(-1, D)
    layer_out, pullback = jax.vjp(forward, tokens_float, params)
    input_grad, grads = pullback(cotangent.astype(jnp.float32))
    return (layer_out.astype(jnp.bfloat16), input_grad, grads[0], grads[1], grads[2], grads[3], grads[4], grads[5], grads[6], grads[7], grads[8], grads[9], grads[10])
```

```python
import functools

import jax
import jax.numpy as jnp
from jax import lax
from jax.experimental import pallas as pl
from jax.experimental.pallas import tpu as pltpu
from jax.sharding import PartitionSpec as P

HEADS = 16
NORM_EPSILON = 1e-05
F32 = jnp.float32
BF16 = jnp.bfloat16

Y, Z, CORES = 2, 4, 2
CHIPS = Y * Z
X, V = 4, 2
OFFSETS = ((0, 0), (0, 1), (0, 3), (1, 0), (0, 2), (1, 1), (1, 3), (1, 2))
WAVES = ((0, 4), (4, 7), (7, 8))
KEY_CHUNK = 512


def shift(value, dy, dz, dc=0):
    pairs = []
    for y in range(Y):
        for z in range(Z):
            for c in range(CORES):
                target = (((y + dy) % Y) * Z + (z + dz) % Z) * CORES + (c + dc) % CORES
                pairs.append(((y * Z + z) * CORES + c, target))
    return lax.ppermute(value, "seq", pairs)


def fetch(value, dy, dz):
    return shift(value, -dy, -dz)


def sibling(value):
    return shift(value, 0, 0, 1)


def dp_shift(value, dv, dx):
    pairs = []
    for v in range(V):
        for x in range(X):
            pairs.append((v * X + x, ((v + dv) % V) * X + (x + dx) % X))
    return lax.ppermute(value, "dp", pairs)


def rows(value, start, stop):
    return lax.slice_in_dim(value, start, stop, axis=0)


def gather_lane(block):
    half = block.shape[0] // 2
    cut_a = block.shape[0] // 4
    cut_b = cut_a + (block.shape[0] - cut_a) // 2
    z_next, z_back, across = fetch(block, 0, 1), fetch(block, 0, -1), fetch(block, 1, 0)
    from_next = fetch(jnp.concatenate([rows(z_next, 0, half), rows(across, half, 2 * half)]), 0, 1)
    from_back = fetch(
        jnp.concatenate([rows(z_back, half, 2 * half), rows(across, half, 2 * half)]), 0, -1
    )
    from_across = fetch(jnp.concatenate([rows(z_next, 0, half), rows(z_back, 0, half)]), 1, 0)
    z_far = jnp.concatenate([rows(from_next, 0, half), rows(from_back, 0, half)])
    across_next = jnp.concatenate([rows(from_across, 0, half), rows(from_next, half, 2 * half)])
    across_back = jnp.concatenate(
        [rows(from_across, half, 2 * half), rows(from_back, half, 2 * half)]
    )
    far_a = fetch(rows(z_far, 0, cut_a), 1, 0)
    far_b = fetch(rows(across_next, cut_a, cut_b), 0, 1)
    far_c = fetch(rows(across_back, cut_b, 2 * half), 0, -1)
    across_far = jnp.concatenate([far_a, far_b, far_c])
    return (block, z_next, z_back, across, z_far, across_next, across_back, across_far)


def scatter_lane(parts):
    own, z_next, z_back, across, z_far, across_next, across_back, across_far = parts
    count = own.shape[0]
    half = count // 2
    cut_a = count // 4
    cut_b = cut_a + (count - cut_a) // 2
    far = across_far.astype(BF16)
    got_a = shift(rows(far, 0, cut_a), 1, 0).astype(F32)
    got_b = shift(rows(far, cut_a, cut_b), 0, 1).astype(F32)
    got_c = shift(rows(far, cut_b, count), 0, -1).astype(F32)
    z_far = jnp.concatenate([rows(z_far, 0, cut_a) + got_a, rows(z_far, cut_a, count)])
    across_next = jnp.concatenate(
        [
            rows(across_next, 0, cut_a),
            rows(across_next, cut_a, cut_b) + got_b,
            rows(across_next, cut_b, count),
        ]
    )
    across_back = jnp.concatenate(
        [rows(across_back, 0, cut_b), rows(across_back, cut_b, count) + got_c]
    )
    to_next = jnp.concatenate([rows(z_far, 0, half), rows(across_next, half, count)])
    to_back = jnp.concatenate([rows(z_far, half, count), rows(across_back, half, count)])
    to_across = jnp.concatenate([rows(across_next, 0, half), rows(across_back, 0, half)])
    got_next = shift(to_next.astype(BF16), 0, 1).astype(F32)
    got_back = shift(to_back.astype(BF16), 0, -1).astype(F32)
    got_across = shift(to_across.astype(BF16), 1, 0).astype(F32)
    z_next = jnp.concatenate(
        [
            rows(z_next, 0, half) + rows(got_next, 0, half) + rows(got_across, 0, half),
            rows(z_next, half, count),
        ]
    )
    z_back = jnp.concatenate(
        [
            rows(z_back, 0, half) + rows(got_across, half, count),
            rows(z_back, half, count) + rows(got_back, 0, half),
        ]
    )
    across = jnp.concatenate(
        [
            rows(across, 0, half),
            rows(across, half, count) + rows(got_next, half, count) + rows(got_back, half, count),
        ]
    )
    return (
        own
        + shift(z_next.astype(BF16), 0, 1).astype(F32)
        + shift(z_back.astype(BF16), 0, -1).astype(F32)
        + shift(across.astype(BF16), 1, 0).astype(F32)
    )


def dp_sum(value):
    x = lax.axis_index("dp") % X
    count = value.shape[0] // X

    def piece(offset):
        return lax.dynamic_slice_in_dim(value, ((x + offset) % X) * count, count, 0)

    total = (
        piece(0).astype(F32)
        + dp_shift(piece(1).astype(BF16), 0, 1).astype(F32)
        + dp_shift(piece(3).astype(BF16), 0, -1).astype(F32)
        + dp_shift(piece(2).astype(BF16), 0, 2).astype(F32)
    )
    total = total + dp_shift(total.astype(BF16), 1, 0).astype(F32)
    low = total.astype(BF16)
    result = jnp.zeros(value.shape, F32)
    parts = (total, dp_shift(low, 0, -1), dp_shift(low, 0, 1), dp_shift(low, 0, 2))
    for offset, part in zip((0, 1, 3, 2), parts):
        result = lax.dynamic_update_slice_in_dim(
            result, part.astype(F32), ((x + offset) % X) * count, 0
        )
    return result


def inverse_rms(values):
    return lax.rsqrt(jnp.mean(values * values, axis=-1, keepdims=True) + NORM_EPSILON)


def rms_back(values, inv_root, gain_row, grad_normed):
    scaled = grad_normed * gain_row
    gain_grad = jnp.sum(grad_normed * values * inv_root, axis=0)
    grad_values = inv_root * scaled - values * inv_root**3 * jnp.mean(
        scaled * values, axis=-1, keepdims=True
    )
    return (grad_values, gain_grad)


def layout(lengths, token_index):
    doc_ends = jnp.cumsum(lengths)
    starts = doc_ends - lengths
    doc_id = jnp.sum((token_index[:, None] >= doc_ends[None, :]).astype(jnp.int32), axis=1)
    numbers = jnp.arange(lengths.shape[0], dtype=jnp.int32)
    doc_start = jnp.sum(jnp.where(doc_id[:, None] == numbers[None, :], starts[None, :], 0), axis=1)
    return doc_start


def rope_tables(position, head_width):
    half_width = head_width // 2
    frequency = 10000.0 ** (-(2.0 * jnp.arange(half_width, dtype=F32)) / head_width)
    angles = position.astype(F32)[:, None] * frequency[None, :]
    return (jnp.cos(angles), jnp.sin(angles))


def rotate(values, cosine, sine):
    half_width = cosine.shape[-1]
    low, high = values[..., :half_width], values[..., half_width:]
    return jnp.concatenate([low * cosine - high * sine, high * cosine + low * sine], axis=-1)


def rotate_back(grads, cosine, sine):
    return rotate(grads, cosine, -sine)


def dot(left, right):
    return jnp.dot(left, right, preferred_element_type=F32)


def dot_nt(left, right):
    return lax.dot_general(left, right, (((1,), (1,)), ((), ())), preferred_element_type=F32)


def dot_tn(left, right):
    return lax.dot_general(left, right, (((0,), (0,)), ((), ())), preferred_element_type=F32)


def order_keys(source_own, source_sib, target, slots, own_lane, width):
    for chip in range(CHIPS):
        slot = slots[chip]
        target[pl.ds(chip * 2 * width + own_lane * width, width), :] = source_own[slot]
        target[pl.ds(chip * 2 * width + (1 - own_lane) * width, width), :] = source_sib[slot]


def masked(scores, first_key, place, begin):
    key = first_key + lax.broadcasted_iota(jnp.int32, scores.shape, 0)
    return jnp.where((key >= begin) & (key <= place), scores, -1e30)


def attend_kernel(
    meta, q_ref, ko_ref, ks_ref, vo_ref, vs_ref, place_ref, begin_ref, out_ref, log_ref, keys, values
):
    width = q_ref.shape[1]
    own_lane = meta[16]
    order_keys(ko_ref, ks_ref, keys, meta, own_lane, width)
    order_keys(vo_ref, vs_ref, values, meta, own_lane, width)
    head = keys.shape[1]

    @pl.loop(0, CHIPS)
    def per_block(block):
        query = jnp.concatenate([q_ref[block, :, :head], q_ref[block, :, head:]], axis=0)
        place, begin = place_ref[block], begin_ref[block]
        last = (meta[8 + block] * 2 + own_lane + 1) * width

        def chunk(step, carry):
            top, total, mixed = carry
            start = pl.multiple_of(step * KEY_CHUNK, KEY_CHUNK)
            key_chunk = keys[pl.ds(start, KEY_CHUNK), :]
            scores = masked(dot_nt(key_chunk, query), start, place, begin)
            new_top = jnp.maximum(top, jnp.max(scores, axis=0, keepdims=True))
            factor = jnp.exp(top - new_top)
            weights = jnp.exp(scores - new_top)
            total = total * factor + jnp.sum(weights, axis=0, keepdims=True)
            mixed = mixed * factor + dot_tn(
                values[pl.ds(start, KEY_CHUNK), :], weights.astype(BF16)
            )
            return (new_top, total, mixed)

        rows_all = query.shape[0]
        top, total, mixed = lax.fori_loop(
            0,
            (last + KEY_CHUNK - 1) // KEY_CHUNK,
            chunk,
            (
                jnp.full((1, rows_all), -1e30, F32),
                jnp.zeros((1, rows_all), F32),
                jnp.zeros((head, rows_all), F32),
            ),
        )
        result = (mixed / total).T.astype(BF16)
        out_ref[block, :, :head] = result[:width]
        out_ref[block, :, head:] = result[width:]
        log_ref[block] = top + jnp.log(total)


def attend_back_kernel(
    meta,
    q_ref,
    ko_ref,
    ks_ref,
    vo_ref,
    vs_ref,
    place_ref,
    begin_ref,
    log_ref,
    out_ref,
    grad_ref,
    gq_ref,
    own_ref,
    sib_ref,
    keys,
    values,
    key_grad,
    value_grad,
):
    width = q_ref.shape[1]
    own_lane = meta[16]
    order_keys(ko_ref, ks_ref, keys, meta, own_lane, width)
    order_keys(vo_ref, vs_ref, values, meta, own_lane, width)
    head = keys.shape[1]
    key_grad[...] = jnp.zeros_like(key_grad)
    value_grad[...] = jnp.zeros_like(value_grad)

    @pl.loop(0, CHIPS)
    def per_block(block):
        query = jnp.concatenate([q_ref[block, :, :head], q_ref[block, :, head:]], axis=0)
        grad = jnp.concatenate([grad_ref[block, :, :head], grad_ref[block, :, head:]], axis=0)
        out = jnp.concatenate([out_ref[block, :, :head], out_ref[block, :, head:]], axis=0)
        row_dot = jnp.sum((grad.astype(F32) * out.astype(F32)).T, axis=0, keepdims=True)
        place, begin, log_total = place_ref[block], begin_ref[block], log_ref[block]
        last = (meta[8 + block] * 2 + own_lane + 1) * width

        def chunk(step, acc):
            start = pl.multiple_of(step * KEY_CHUNK, KEY_CHUNK)
            span = pl.ds(start, KEY_CHUNK)
            key_chunk = keys[span, :]
            scores = masked(dot_nt(key_chunk, query), start, place, begin)
            probs = jnp.exp(scores - log_total)
            grad_probs = dot_nt(values[span, :], grad)
            grad_scores = (probs * (grad_probs - row_dot)).astype(BF16)
            value_grad[span, :] += dot(probs.astype(BF16), grad)
            key_grad[span, :] += dot(grad_scores, query)
            return acc + dot_tn(grad_scores, key_chunk)

        acc = lax.fori_loop(
            0,
            (last + KEY_CHUNK - 1) // KEY_CHUNK,
            chunk,
            jnp.zeros((query.shape[0], head), F32),
        )
        acc = acc * (head**-0.5)
        gq_ref[block, :, :head] = acc[:width]
        gq_ref[block, :, head:] = acc[width:]

    for chip in range(CHIPS):
        slot = meta[chip]
        own_rows = pl.ds(chip * 2 * width + own_lane * width, width)
        sib_rows = pl.ds(chip * 2 * width + (1 - own_lane) * width, width)
        own_ref[slot, :, :head] = key_grad[own_rows, :]
        own_ref[slot, :, head:] = value_grad[own_rows, :]
        sib_ref[slot, :, :head] = key_grad[sib_rows, :].astype(BF16)
        sib_ref[slot, :, head:] = value_grad[sib_rows, :].astype(BF16)


def kernel_specs(count):
    smem = pl.BlockSpec(memory_space=pltpu.SMEM)
    vmem = pl.BlockSpec(memory_space=pltpu.VMEM)
    return [smem] + [vmem] * count


def attend(meta, queries, key_own, key_sib, value_own, value_sib, place, begin):
    width, head = queries.shape[1], key_own.shape[2]
    group = CHIPS * CORES * width
    return pl.pallas_call(
        attend_kernel,
        out_shape=(
            jax.ShapeDtypeStruct(queries.shape, BF16),
            jax.ShapeDtypeStruct(place.shape, F32),
        ),
        in_specs=kernel_specs(7),
        out_specs=tuple(kernel_specs(2)[1:]),
        scratch_shapes=[pltpu.VMEM((group, head), BF16)] * 2,
        compiler_params=pltpu.CompilerParams(vmem_limit_bytes=40 * 2**20),
        cost_estimate=pl.CostEstimate(
            flops=2_600_000_000, bytes_accessed=5_000_000, transcendentals=2_600_000
        ),
        name="attend",
    )(meta, queries, key_own, key_sib, value_own, value_sib, place, begin)


def attend_back(meta, queries, key_own, key_sib, value_own, value_sib, place, begin, log, out, grad):
    width, head = queries.shape[1], key_own.shape[2]
    group = CHIPS * CORES * width
    return pl.pallas_call(
        attend_back_kernel,
        out_shape=(
            jax.ShapeDtypeStruct(queries.shape, F32),
            jax.ShapeDtypeStruct((CHIPS, width, 2 * head), F32),
            jax.ShapeDtypeStruct((CHIPS, width, 2 * head), BF16),
        ),
        in_specs=kernel_specs(10),
        out_specs=tuple(kernel_specs(3)[1:]),
        scratch_shapes=[pltpu.VMEM((group, head), BF16)] * 2 + [pltpu.VMEM((group, head), F32)] * 2,
        compiler_params=pltpu.CompilerParams(vmem_limit_bytes=48 * 2**20),
        cost_estimate=pl.CostEstimate(
            flops=6_500_000_000, bytes_accessed=10_000_000, transcendentals=2_600_000
        ),
        name="attend_back",
    )(meta, queries, key_own, key_sib, value_own, value_sib, place, begin, log, out, grad)


def shards(
    tokens,
    doc_lengths,
    first_gain,
    query_down,
    key_proj,
    value_proj,
    query_gain,
    query_up,
    out_proj,
    second_gain,
    gate_proj,
    up_proj,
    down_proj,
    cotangent,
):
    width, model = tokens.shape
    latent_width = query_down.shape[1]
    head = key_proj.shape[1]
    hidden_width = gate_proj.shape[1] // (CHIPS * CORES)
    small_width = 128
    lane_width = latent_width + 2 * head

    me = lax.axis_index("seq")
    core = me % CORES
    chip = me // CORES
    z, y = chip % Z, chip // Z
    chip_at = [((y + dy) % Y) * Z + (z + dz) % Z for dy, dz in OFFSETS]

    gains = jnp.stack(
        [first_gain, second_gain, jnp.pad(query_gain, (0, width - query_gain.shape[0]))], axis=1
    )
    packed = jnp.concatenate(
        [query_down, key_proj, value_proj, jnp.pad(gains, ((0, 0), (0, small_width - 3)))], axis=1
    )
    weights = lax.all_gather(packed, "seq", axis=0, tiled=True)

    def swap(weight):
        depth = weight.shape[0]
        parts = weight.reshape(depth, CHIPS * CORES, -1).transpose(1, 0, 2)
        return lax.all_to_all(parts, "seq", 0, 0).reshape(CHIPS * CORES * depth, -1)

    up_own = swap(query_up)
    gate_lift_own = swap(
        jnp.concatenate(
            [
                gate_proj.reshape(width, CHIPS * CORES, hidden_width),
                up_proj.reshape(width, CHIPS * CORES, hidden_width),
            ],
            axis=2,
        )
    )
    query_up_chip = jnp.concatenate([up_own, sibling(up_own)], axis=1)
    out_chip = jnp.concatenate([out_proj, sibling(out_proj)], axis=0)
    gate_lift_sib = sibling(gate_lift_own)
    gate_chip = jnp.concatenate(
        [gate_lift_own[:, :hidden_width], gate_lift_sib[:, :hidden_width]], axis=1
    )
    lift_chip = jnp.concatenate(
        [gate_lift_own[:, hidden_width:], gate_lift_sib[:, hidden_width:]], axis=1
    )
    down_chip = jnp.concatenate([down_proj, sibling(down_proj)], axis=0)

    lengths = doc_lengths[0]
    blocks = jnp.stack([place * CORES + core for place in chip_at])
    token_index = blocks[:, None] * width + jnp.arange(width, dtype=jnp.int32)[None, :]
    doc_start = layout(lengths, token_index.reshape(-1)).reshape(token_index.shape)
    cosine, sine = rope_tables((token_index - doc_start).reshape(-1), head)
    slot_of = [
        sum(jnp.where(chip_at[slot] == number, slot, 0) for slot in range(CHIPS))
        for number in range(CHIPS)
    ]
    meta = jnp.stack(slot_of + chip_at + [core]).astype(jnp.int32)
    place_row = jnp.tile(token_index, (1, 2))[:, None, :]
    begin_row = jnp.tile(doc_start, (1, 2))[:, None, :]

    tokens_float = tokens.astype(F32)
    inv_one = inverse_rms(tokens_float)
    gain_rows = weights[:, lane_width : lane_width + 3].astype(F32).T
    gain_one, gain_two = gain_rows[0:1], gain_rows[1:2]
    gain_query = gain_rows[2].reshape(-1, width)[:, : query_gain.shape[0]].reshape(1, -1)
    normed = (tokens_float * inv_one * gain_one).astype(BF16)
    first = dot(normed, weights)
    latent = first[:, :latent_width]
    inv_latent = inverse_rms(latent)
    latent_n = (latent * inv_latent * gain_query).astype(BF16)
    cos_own, sin_own = cosine[:width], sine[:width]
    key_rot = rotate(first[:, latent_width : latent_width + head], cos_own, sin_own).astype(BF16)
    value_low = first[:, latent_width + head : lane_width].astype(BF16)

    lane = gather_lane(jnp.concatenate([latent_n, key_rot, value_low], axis=1))
    lane_all = jnp.concatenate(lane, axis=0)
    latent_lane = lane_all[:, :latent_width]
    key_value_own = lane_all[:, latent_width:]
    key_value_sib = sibling(key_value_own).reshape(CHIPS, width, 2 * head)
    key_value_own = key_value_own.reshape(CHIPS, width, 2 * head)
    key_own, value_own = key_value_own[..., :head], key_value_own[..., head:]
    key_sib, value_sib = key_value_sib[..., :head], key_value_sib[..., head:]

    queries = dot(latent_lane, query_up_chip).reshape(CHIPS * width, 2, head)
    query_rot = rotate(queries, cosine[:, None, :], sine[:, None, :]) * head**-0.5
    query_rot = query_rot.astype(BF16).reshape(CHIPS, width, 2 * head)
    attended, log_total = attend(
        meta, query_rot, key_own, key_sib, value_own, value_sib, place_row, begin_row
    )
    attended_rows = attended.reshape(CHIPS * width, 2 * head)
    mixed = dot(attended_rows, out_chip).reshape(CHIPS, width, model)
    residual = tokens_float + scatter_lane([mixed[i] for i in range(CHIPS)])
    inv_two = inverse_rms(residual)
    normed_two = (residual * inv_two * gain_two).astype(BF16)

    cot_lane = gather_lane(cotangent)
    normed_lane = gather_lane(normed_two)
    wave_values = []
    fed, back = [], []
    for first_block, last_block in WAVES:
        normed_wave = jnp.concatenate(normed_lane[first_block:last_block], axis=0)
        cot_wave = jnp.concatenate(cot_lane[first_block:last_block], axis=0)
        gate_values = dot(normed_wave, gate_chip)
        up_values = dot(normed_wave, lift_chip)
        grad_hidden = dot_nt(cot_wave, down_chip)
        sigmoid = jax.nn.sigmoid(gate_values)
        hidden = (gate_values * sigmoid * up_values).astype(BF16)
        grad_gate = (
            grad_hidden * up_values * sigmoid * (1.0 + gate_values * (1.0 - sigmoid))
        ).astype(BF16)
        grad_up = (grad_hidden * gate_values * sigmoid).astype(BF16)
        wave_values.append((normed_wave, cot_wave, hidden, grad_gate, grad_up))
        back_wave = dot_nt(grad_gate, gate_chip) + dot_nt(grad_up, lift_chip)
        fed_wave = dot(hidden, down_chip)
        for block in range(last_block - first_block):
            back.append(rows(back_wave, block * width, (block + 1) * width))
            fed.append(rows(fed_wave, block * width, (block + 1) * width))
    grad_normed_two = scatter_lane(back)
    layer_out = (residual + scatter_lane(fed)).astype(BF16)
    normed_two_all, cot_all, hidden_all, grad_gate_all, grad_up_all = (
        jnp.concatenate([wave[i] for wave in wave_values], axis=0) for i in range(5)
    )
    gate_grad = dot_tn(normed_two_all, grad_gate_all)
    lift_grad = dot_tn(normed_two_all, grad_up_all)
    down_grad = dot_tn(hidden_all, cot_all)

    grad_two, second_grad = rms_back(residual, inv_two, gain_two, grad_normed_two)
    grad_residual = cotangent.astype(F32) + grad_two

    branch_all = jnp.concatenate(gather_lane(grad_residual.astype(BF16)), axis=0)
    grad_attended = dot_nt(branch_all, out_chip).astype(BF16).reshape(CHIPS, width, 2 * head)
    out_grad = dot_tn(attended_rows, branch_all)
    grad_qrot, key_value_grad, key_value_grad_sib = attend_back(
        meta,
        query_rot,
        key_own,
        key_sib,
        value_own,
        value_sib,
        place_row,
        begin_row,
        log_total,
        attended,
        grad_attended,
    )
    key_value_grad = key_value_grad + sibling(key_value_grad_sib).astype(F32)
    grad_queries = rotate_back(
        grad_qrot.reshape(CHIPS * width, 2, head), cosine[:, None, :], sine[:, None, :]
    )
    grad_queries = grad_queries.astype(BF16).reshape(CHIPS * width, 2 * head)
    up_grad = dot_tn(latent_lane, grad_queries)
    latent_parts = dot_nt(grad_queries, query_up_chip).reshape(CHIPS, width, latent_width)
    summed = scatter_lane(
        [jnp.concatenate([latent_parts[i], key_value_grad[i]], axis=1) for i in range(CHIPS)]
    )
    grad_keys = rotate_back(
        summed[:, latent_width : latent_width + head], cos_own, sin_own
    ).astype(BF16)
    grad_values = summed[:, latent_width + head :].astype(BF16)
    grad_latent, query_gain_grad = rms_back(
        latent, inv_latent, gain_query, summed[:, :latent_width]
    )
    grad_first = jnp.concatenate([grad_latent.astype(BF16), grad_keys, grad_values], axis=1)
    grad_normed = dot_nt(jnp.pad(grad_first, ((0, 0), (0, small_width))), weights)
    grad_one, first_grad = rms_back(tokens_float, inv_one, gain_one, grad_normed)
    input_grad = grad_residual + grad_one

    count = CHIPS * CORES
    gain_grads = jnp.concatenate(
        [
            first_grad.reshape(count, -1),
            second_grad.reshape(count, -1),
            query_gain_grad.reshape(count, -1),
        ],
        axis=1,
    )
    gain_cols = gain_grads.size // width
    gain_grads = gain_grads.reshape(width, gain_cols).astype(BF16)
    first_lane = jnp.concatenate(
        gather_lane(
            jnp.concatenate(
                [grad_first, jnp.pad(gain_grads, ((0, 0), (0, small_width - gain_cols)))], axis=1
            )
        ),
        axis=0,
    )
    columns = []
    for dy, dz in OFFSETS:
        wanted = ((y - dy) % Y) * Z + (z - dz) % Z
        part = lax.dynamic_slice_in_dim(normed, wanted * 2 * width, 2 * width, 1)
        columns.append(part if (dy, dz) == (0, 0) else fetch(part, dy, dz))
    first_weights = dot_tn(jnp.concatenate(columns, axis=0), first_lane)
    gain_sums = jnp.sum(
        first_lane[:, lane_width : lane_width + gain_cols]
        .astype(F32)
        .reshape(CHIPS, width, gain_cols),
        axis=0,
    )
    gain_sums = gain_sums + sibling(gain_sums)
    own_first = lax.dynamic_slice_in_dim(first_weights, core * width, width, 0)
    sib_first = lax.dynamic_slice_in_dim(first_weights, (1 - core) * width, width, 0)
    own_first = own_first + sibling(sib_first.astype(BF16)).astype(F32)
    own_gains = lax.dynamic_slice_in_dim(gain_sums, me * (width // count), width // count, 0)
    tail = dp_sum(
        jnp.concatenate(
            [
                own_first[:, :lane_width],
                jnp.pad(
                    own_gains, ((0, width - width // count), (0, small_width - gain_cols))
                ),
            ],
            axis=1,
        )
    )
    own_gains = tail[: width // count, lane_width : lane_width + gain_cols].reshape(-1)

    def combine(grad, axis):
        size = grad.shape[axis] // 2
        own = lax.slice_in_dim(grad, 0, size, axis=axis)
        other = lax.slice_in_dim(grad, size, 2 * size, axis=axis)
        return own + sibling(other.astype(BF16)).astype(F32)

    def swap_back(grad):
        depth = grad.shape[0] // count
        parts = lax.all_to_all(grad.astype(BF16).reshape(count, depth, -1), "seq", 0, 0)
        return parts

    gate_lift_grad = jnp.concatenate([combine(gate_grad, 1), combine(lift_grad, 1)], axis=1)
    gate_lift_grad = swap_back(gate_lift_grad)
    gate_own = gate_lift_grad[..., :hidden_width].transpose(1, 0, 2).reshape(width, -1)
    lift_own = gate_lift_grad[..., hidden_width:].transpose(1, 0, 2).reshape(width, -1)
    up_own_grad = swap_back(combine(up_grad, 1))
    up_own_grad = up_own_grad.transpose(1, 0, 2).reshape(query_up.shape)
    gate_sum, lift_sum, down_sum = lax.psum(
        (gate_own, lift_own, combine(down_grad, 0).astype(BF16)), "dp"
    )
    out_sum, up_sum = lax.psum((combine(out_grad, 0).astype(BF16), up_own_grad), "dp")

    def wide(value):
        return value.astype(F32)

    return (
        layer_out,
        input_grad,
        own_gains[:width],
        tail[:, :latent_width],
        tail[:, latent_width : latent_width + head],
        tail[:, latent_width + head : lane_width],
        own_gains[2 * width :],
        wide(up_sum),
        wide(out_sum),
        own_gains[width : 2 * width],
        wide(gate_sum),
        wide(lift_sum),
        wide(down_sum),
    )


def solution(mesh):
    split = P(("dp", "seq"), None)
    matrix, vector = P("seq", None), P("seq")
    in_specs = (
        split,
        P("dp", None),
        vector,
        matrix,
        matrix,
        matrix,
        vector,
        matrix,
        matrix,
        vector,
        matrix,
        matrix,
        matrix,
        split,
    )
    out_specs = (
        split,
        split,
        vector,
        matrix,
        matrix,
        matrix,
        vector,
        matrix,
        matrix,
        vector,
        matrix,
        matrix,
        matrix,
    )
    return jax.shard_map(shards, mesh=mesh, in_specs=in_specs, out_specs=out_specs, check_vma=False)
```

```python
import jax
import jax.numpy as jnp
from jax import lax
from jax.experimental import pallas as pl
from jax.experimental.pallas import tpu as pltpu
from jax.sharding import Mesh, PartitionSpec as P

NORM_EPSILON = 1e-05
F32 = jnp.float32
BF16 = jnp.bfloat16

AXES = ("v", "x", "y", "z", "c")
SIZES = (2, 4, 2, 4, 2)
DP, SEQ, ACROSS = ("v", "x"), ("y", "z", "c"), ("v", "x", "y")
SLOT = 384
KEY_CHUNK = 512


def turn(value, axis, step):
    size = SIZES[AXES.index(axis)]
    return lax.ppermute(value, axis, [(i, (i + step) % size) for i in range(size)])


def sibling(value):
    return turn(value, "c", 1)


def after(value, other):
    first = other[(0,) * other.ndim] if other.ndim else other
    return value + (first * 0).astype(value.dtype)


def rows(value, start, stop):
    return lax.slice_in_dim(value, start, stop, axis=0)


def exchange(parts, axes):
    return lax.all_to_all(parts, axes, 0, 0)


def spread(value, axes):
    count = 1
    for axis in axes:
        count *= SIZES[AXES.index(axis)]
    return exchange(jnp.broadcast_to(value[None], (count,) + value.shape), axes)


def total_of(parts):
    return jnp.sum(parts.astype(F32), axis=0)


def ring_gather(block, axis="z"):
    half = block.shape[0] // 2
    after_it, before_it = turn(block, axis, -1), turn(block, axis, 1)
    far_low = turn(rows(after_it, 0, half), axis, -1)
    far_high = turn(rows(before_it, half, 2 * half), axis, 1)
    return (block, far_low, far_high, after_it, before_it)


def ring_merge_kernel(part_ref, low_ref, high_ref, next_ref, back_ref):
    half = low_ref.shape[0]
    next_ref[half:, :] = part_ref[0, half:, :]
    next_ref[:half, :] = (part_ref[0, :half, :].astype(F32) + low_ref[...].astype(F32)).astype(BF16)
    back_ref[:half, :] = part_ref[1, :half, :]
    back_ref[half:, :] = (part_ref[1, half:, :].astype(F32) + high_ref[...].astype(F32)).astype(
        BF16
    )


def ring_scatter(parts, other=None):
    _, width, size = parts.shape
    half = width // 2
    got_low = turn(parts[1, :half], "z", 1)
    got_high = turn(parts[1, half:], "z", -1)
    if other is not None:
        got_low = after(got_low, other)
    half_spec = pl.BlockSpec((half, size), lambda i: (0, 0))
    full_spec = pl.BlockSpec((width, size), lambda i: (0, 0))
    to_next, to_back = pl.pallas_call(
        ring_merge_kernel,
        grid=(1,),
        out_shape=(jax.ShapeDtypeStruct((width, size), BF16),) * 2,
        in_specs=[pl.BlockSpec((2, width, size), lambda i: (1, 0, 0)), half_spec, half_spec],
        out_specs=(full_spec, full_spec),
        name="ring_merge",
    )(parts, got_low, got_high)
    return (
        parts[0].astype(F32)
        + turn(to_next, "z", 1).astype(F32)
        + turn(to_back, "z", -1).astype(F32)
    )


def inverse_rms(values):
    return lax.rsqrt(jnp.mean(values * values, axis=-1, keepdims=True) + NORM_EPSILON)


def rms_back(values, inv_root, gain_row, grad_normed):
    scaled = grad_normed * gain_row
    return inv_root * scaled - values * inv_root**3 * jnp.mean(
        scaled * values, axis=-1, keepdims=True
    )


def layout(lengths, token_index):
    doc_ends = jnp.cumsum(lengths)
    starts = doc_ends - lengths
    doc_id = jnp.sum((token_index[:, None] >= doc_ends[None, :]).astype(jnp.int32), axis=1)
    numbers = jnp.arange(lengths.shape[0], dtype=jnp.int32)
    doc_start = jnp.sum(jnp.where(doc_id[:, None] == numbers[None, :], starts[None, :], 0), axis=1)
    return doc_start


def rope_tables(position, head_width):
    half_width = head_width // 2
    frequency = 10000.0 ** (-(2.0 * jnp.arange(half_width, dtype=F32)) / head_width)
    angles = position.astype(F32)[:, None] * frequency[None, :]
    return (jnp.cos(angles), jnp.sin(angles))


def rotate(values, cosine, sine):
    half_width = cosine.shape[-1]
    low, high = values[..., :half_width], values[..., half_width:]
    return jnp.concatenate([low * cosine - high * sine, high * cosine + low * sine], axis=-1)


def rotate_back(grads, cosine, sine):
    return rotate(grads, cosine, -sine)


def dot(left, right):
    return jnp.dot(left, right, preferred_element_type=F32)


def dot_nt(left, right):
    return lax.dot_general(left, right, (((1,), (1,)), ((), ())), preferred_element_type=F32)


def dot_tn(left, right):
    return lax.dot_general(left, right, (((0,), (0,)), ((), ())), preferred_element_type=F32)


def masked(scores, first_key, place, begin):
    key = first_key + lax.broadcasted_iota(jnp.int32, scores.shape, 0)
    return jnp.where((key >= begin) & (key <= place), scores, -1e30)


def chunk_bounds(meta, block, width):
    number = meta[6 + block]
    count = ((number + 1) * width + KEY_CHUNK - 1) // KEY_CHUNK
    clear_from = jnp.minimum((meta[2 + block] + KEY_CHUNK - 1) // KEY_CHUNK, count)
    clear_to = jnp.maximum((number * width + 1) // KEY_CHUNK, clear_from)
    return clear_from, clear_to, count


def stack_lane(refs):
    return jnp.concatenate([ref[...] for ref in refs], axis=0)


def stack_heads(ref, block, first, head):
    return jnp.concatenate(
        [ref[block, :, first : first + head], ref[block, :, first + head : first + 2 * head]],
        axis=0,
    )


def query_kernel(lane_a, lane_b, lane_c, lane_d, lane_e, up_ref, cos_ref, sin_ref, q_ref):
    blocks, width, size = q_ref.shape
    half = cos_ref.shape[1]
    head = 2 * half
    latent = stack_lane((lane_a, lane_b, lane_c, lane_d, lane_e))
    cosine, sine = cos_ref[...], sin_ref[...]
    for start in range(0, size, head):
        query = dot(latent, up_ref[:, start : start + head])
        low, high = query[:, :half], query[:, half:]
        turned = ((low * cosine - high * sine), (high * cosine + low * sine))
        for part, value in enumerate(turned):
            q_ref[:, :, start + part * half : start + (part + 1) * half] = (
                (value * head**-0.5).astype(BF16).reshape(blocks, width, half)
            )


def attend_kernel(meta, q_ref, kv_ref, place_ref, begin_ref, out_ref, log_ref):
    blocks, width, size = q_ref.shape
    head = kv_ref.shape[1] // 2
    pairs = range(size // head // 2)

    @pl.loop(0, blocks)
    def per_block(block):
        clear_from, clear_to, count = chunk_bounds(meta, block, width)
        place, begin = place_ref[block], begin_ref[block]
        queries = [stack_heads(q_ref, block, pair * 2 * head, head) for pair in pairs]

        def chunk(step, carries, clear):
            start = pl.multiple_of(step * KEY_CHUNK, KEY_CHUNK)
            key_chunk = kv_ref[pl.ds(start, KEY_CHUNK), :head]
            value_chunk = kv_ref[pl.ds(start, KEY_CHUNK), head:]
            result = []
            for query, (top, total, mixed) in zip(queries, carries):
                scores = dot_nt(key_chunk, query)
                if not clear:
                    scores = masked(scores, start, place, begin)
                new_top = jnp.maximum(top, jnp.max(scores, axis=0, keepdims=True))
                factor = jnp.exp(top - new_top)
                weights = jnp.exp(scores - new_top)
                total = total * factor + jnp.sum(weights, axis=0, keepdims=True)
                mixed = mixed * factor + dot_tn(value_chunk, weights.astype(BF16))
                result.append((new_top, total, mixed))
            return tuple(result)

        carry = tuple(
            (
                jnp.full((1, 2 * width), -1e30, F32),
                jnp.zeros((1, 2 * width), F32),
                jnp.zeros((head, 2 * width), F32),
            )
            for _ in pairs
        )
        carry = lax.fori_loop(0, clear_from, lambda s, w: chunk(s, w, False), carry)
        carry = lax.fori_loop(clear_from, clear_to, lambda s, w: chunk(s, w, True), carry)
        carry = lax.fori_loop(clear_to, count, lambda s, w: chunk(s, w, False), carry)
        for pair, (top, total, mixed) in zip(pairs, carry):
            first = pair * 2 * head
            result = (mixed / total).T.astype(BF16)
            out_ref[block, :, first : first + head] = result[:width]
            out_ref[block, :, first + head : first + 2 * head] = result[width:]
            log_ref[block, pair] = top + jnp.log(total)


def attend_back_kernel(
    meta,
    branch_a,
    branch_b,
    branch_c,
    branch_d,
    branch_e,
    kv_ref,
    up_ref,
    proj_a,
    proj_b,
    proj_c,
    proj_d,
    cos_ref,
    sin_ref,
    place_ref,
    begin_ref,
    q_ref,
    out_ref,
    log_ref,
    lane_a,
    lane_b,
    lane_c,
    lane_d,
    lane_e,
    gq_ref,
    latent_ref,
    kv_own,
    kv_sib,
    out_own,
    out_sib,
    up_own,
    up_sib,
    grads,
    key_grad,
    value_grad,
):
    blocks, width, _ = q_ref.shape
    head = kv_ref.shape[1] // 2
    half = head // 2
    heads = q_ref.shape[2] // head
    branch = stack_lane((branch_a, branch_b, branch_c, branch_d, branch_e))
    y = meta[0]
    for at, (ref, yy) in enumerate(
        ((proj_a, y), (proj_b, 1 - y), (proj_c, y), (proj_d, 1 - y))
    ):
        first = pl.multiple_of((at // 2 * 2 + yy) * head, head)
        value = dot_nt(branch, ref[...])
        grads[:, :, pl.ds(first, head)] = value.astype(BF16).reshape(blocks, width, head)
    key_grad[...] = jnp.zeros_like(key_grad)
    value_grad[...] = jnp.zeros_like(value_grad)

    pairs = range(heads // 2)

    @pl.loop(0, blocks)
    def per_block(block):
        clear_from, clear_to, count = chunk_bounds(meta, block, width)
        place, begin = place_ref[block], begin_ref[block]
        token = pl.ds(pl.multiple_of(block * width, width), width)
        cosine, sine = cos_ref[token, :], sin_ref[token, :]
        fixed = []
        for pair in pairs:
            query, grad, out = (
                stack_heads(ref, block, pair * 2 * head, head) for ref in (q_ref, grads, out_ref)
            )
            row_dot = jnp.sum((grad.astype(F32) * out.astype(F32)).T, axis=0, keepdims=True)
            fixed.append((query, grad, row_dot, log_ref[block, pair]))

        def chunk(step, accs, clear):
            start = pl.multiple_of(step * KEY_CHUNK, KEY_CHUNK)
            span = pl.ds(start, KEY_CHUNK)
            key_chunk, value_chunk = kv_ref[span, :head], kv_ref[span, head:]
            key_sum, value_sum = key_grad[span, :], value_grad[span, :]
            result = []
            for (query, grad, row_dot, log_total), acc in zip(fixed, accs):
                scores = dot_nt(key_chunk, query)
                if not clear:
                    scores = masked(scores, start, place, begin)
                probs = jnp.exp(scores - log_total)
                grad_probs = dot_nt(value_chunk, grad)
                grad_scores = (probs * (grad_probs - row_dot)).astype(BF16)
                value_sum += dot(probs.astype(BF16), grad)
                key_sum += dot(grad_scores, query)
                result.append(acc + dot_tn(grad_scores, key_chunk))
            key_grad[span, :] = key_sum
            value_grad[span, :] = value_sum
            return tuple(result)

        accs = tuple(jnp.zeros((2 * width, head), F32) for _ in pairs)
        accs = lax.fori_loop(0, clear_from, lambda s, w: chunk(s, w, False), accs)
        accs = lax.fori_loop(clear_from, clear_to, lambda s, w: chunk(s, w, True), accs)
        accs = lax.fori_loop(clear_to, count, lambda s, w: chunk(s, w, False), accs)
        for pair, acc in zip(pairs, accs):
            acc = acc * (head**-0.5)
            for h in range(2):
                value = acc[h * width : (h + 1) * width]
                low, high = value[:, :half], value[:, half:]
                start = (pair * 2 + h) * head
                gq_ref[block, :, start : start + half] = (low * cosine + high * sine).astype(BF16)
                gq_ref[block, :, start + half : start + head] = (
                    high * cosine - low * sine
                ).astype(BF16)

    grad_query = gq_ref[...].reshape(blocks * width, heads * head)
    size = latent_ref.shape[2]
    piece = 256
    for start in range(0, size, piece):
        value = dot_nt(grad_query, up_ref[start : start + piece, :])
        latent_ref[:, :, start : start + piece] = value.astype(BF16).reshape(blocks, width, piece)
    mixed = out_ref[...].reshape(blocks * width, heads * head)
    latent = stack_lane((lane_a, lane_b, lane_c, lane_d, lane_e))
    for h in range(heads):
        span = slice(h * head, (h + 1) * head)
        at = slice((h % 2) * head, (h % 2 + 1) * head)
        target = (out_own, out_sib)[h // 2]
        target[at, :] = dot_tn(mixed[:, span], branch).astype(BF16)
        target = (up_own, up_sib)[h // 2]
        target[:, at] = dot_tn(latent, grad_query[:, span]).astype(BF16)
    c = meta[1]
    for chip in range(2 * blocks):
        for target, cc in ((kv_own, c), (kv_sib, 1 - c)):
            span = pl.ds(pl.multiple_of((chip * 2 + cc) * width, width), width)
            target[chip, :, :head] = key_grad[span, :].astype(BF16)
            target[chip, :, head:] = value_grad[span, :].astype(BF16)


def kernel_specs(count):
    smem = pl.BlockSpec(memory_space=pltpu.SMEM)
    vmem = pl.BlockSpec(memory_space=pltpu.VMEM)
    return [smem] + [vmem] * count


def column_kernel(meta, normed_ref, *targets):
    width = targets[0].shape[0]
    z, c = meta[0], meta[1]
    for step, target in zip((0, 2, 1, 3), targets):
        place = (z + 4 - step) % 4
        for at, (cc, y) in enumerate(((c, 0), (c, 1), (1 - c, 0), (1 - c, 1))):
            start = pl.multiple_of(((y * 4 + place) * 2 + cc) * width, width)
            target[:, at * width : (at + 1) * width] = normed_ref[:, pl.ds(start, width)]


def first_kernel(col_a, col_b, col_c, col_d, g_a, g_b, g_c, g_d, g_e, own_ref, other_ref):
    columns = stack_lane((col_a, col_b, col_c, col_d))
    grads = stack_lane((g_a, g_b, g_c, g_d, g_e))
    half = own_ref.shape[0]
    own_ref[...] = dot_tn(columns[:, :half], grads)
    other_ref[...] = dot_tn(columns[:, half:], grads).astype(BF16)


def first_weights(columns, lane):
    half, size = columns[0].shape[1] // 2, lane[0].shape[1]
    return pl.pallas_call(
        first_kernel,
        out_shape=(
            jax.ShapeDtypeStruct((half, size), F32),
            jax.ShapeDtypeStruct((half, size), BF16),
        ),
        in_specs=kernel_specs(9)[1:],
        out_specs=tuple(kernel_specs(2)[1:]),
        compiler_params=pltpu.CompilerParams(vmem_limit_bytes=16 * 2**20),
        cost_estimate=pl.CostEstimate(
            flops=800_000_000, bytes_accessed=5_000_000, transcendentals=0
        ),
        name="first_weights",
    )(*columns, *lane)


def pick_columns(normed, z, c):
    width = normed.shape[0]
    return pl.pallas_call(
        column_kernel,
        out_shape=(jax.ShapeDtypeStruct((width, 4 * width), BF16),) * 4,
        in_specs=kernel_specs(1),
        out_specs=tuple(kernel_specs(4)[1:]),
        name="pick_columns",
    )(jnp.stack([z, c]).astype(jnp.int32), normed)


def make_queries(lane, up, cosine, sine, blocks):
    width = lane[0].shape[0]
    return pl.pallas_call(
        query_kernel,
        out_shape=jax.ShapeDtypeStruct((blocks, width, up.shape[1]), BF16),
        in_specs=kernel_specs(8)[1:],
        out_specs=kernel_specs(1)[1],
        compiler_params=pltpu.CompilerParams(vmem_limit_bytes=24 * 2**20),
        cost_estimate=pl.CostEstimate(
            flops=1_100_000_000, bytes_accessed=5_000_000, transcendentals=0
        ),
        name="make_queries",
    )(*lane, up, cosine, sine)


def attend(meta, query, kv, place, begin):
    blocks, width, size = query.shape
    head = kv.shape[1] // 2
    shape = jax.ShapeDtypeStruct
    return pl.pallas_call(
        attend_kernel,
        out_shape=(
            shape(query.shape, BF16),
            shape((blocks, size // head // 2, 1, 2 * width), F32),
        ),
        in_specs=kernel_specs(4),
        out_specs=tuple(kernel_specs(2)[1:]),
        compiler_params=pltpu.CompilerParams(vmem_limit_bytes=32 * 2**20),
        cost_estimate=pl.CostEstimate(
            flops=20_000_000_000, bytes_accessed=5_000_000, transcendentals=3_400_000
        ),
        name="attend",
    )(meta, query, kv, place, begin)


def project_kernel(meta, mixed_ref, own_ref, across_ref, sib_ref, across_sib_ref, part_ref):
    blocks, width, model = part_ref.shape
    head = own_ref.shape[0]
    y = meta[0]
    piece = 512
    for start in range(0, model, piece):
        total = None
        for at, (ref, yy) in enumerate(
            ((own_ref, y), (across_ref, 1 - y), (sib_ref, y), (across_sib_ref, 1 - y))
        ):
            first = pl.multiple_of((at // 2 * 2 + yy) * head, head)
            left = mixed_ref[:, :, pl.ds(first, head)].reshape(blocks * width, head)
            value = dot(left, ref[:, start : start + piece])
            total = value if total is None else total + value
        part_ref[:, :, start : start + piece] = total.astype(BF16).reshape(blocks, width, piece)


def project(meta, mixed, pieces):
    blocks, width, _ = mixed.shape
    model = pieces[0].shape[1]
    return pl.pallas_call(
        project_kernel,
        out_shape=jax.ShapeDtypeStruct((blocks, width, model), BF16),
        in_specs=kernel_specs(5),
        out_specs=kernel_specs(1)[1],
        compiler_params=pltpu.CompilerParams(vmem_limit_bytes=24 * 2**20),
        cost_estimate=pl.CostEstimate(
            flops=2_200_000_000, bytes_accessed=7_500_000, transcendentals=0
        ),
        name="project",
    )(meta, mixed, *pieces)


def feed_kernel(n_ref, cot_ref, own_ref, sib_ref, down_ref, hid_ref, go_ref, gs_ref, back_ref):
    slot = down_ref.shape[0] // 2
    blocks, _, size = own_ref.shape
    normed = n_ref[...]
    grad_hidden = dot_nt(cot_ref[...], down_ref[...])
    back = None
    for at, (weight, grad_ref) in enumerate(((own_ref, go_ref), (sib_ref, gs_ref))):
        span = slice(at * slot, (at + 1) * slot)
        both = jnp.concatenate([dot(normed, weight[i]) for i in range(blocks)], axis=1)
        gate, lift = both[:, :slot], both[:, slot:]
        grad = grad_hidden[:, span]
        sigmoid = jax.nn.sigmoid(gate)
        active = gate * sigmoid
        hid_ref[:, span] = (active * lift).astype(BF16)
        grad_ref[:, :slot] = (grad * lift * sigmoid * (1.0 + gate * (1.0 - sigmoid))).astype(BF16)
        grad_ref[:, slot:] = (grad * active).astype(BF16)
        for i in range(blocks):
            part = dot_nt(grad_ref[:, i * size : (i + 1) * size], weight[i])
            back = part if back is None else back + part
    back_ref[...] = back.astype(BF16)


def combine_kernel(feed_ref, feed_got, down_ref, down_got, out_ref):
    parts, owners, quarter, _ = out_ref.shape
    wide = feed_ref.shape[1]
    for owner in range(owners):
        for x in range(parts):
            span = slice((owner * parts + x) * quarter, (owner * parts + x + 1) * quarter)
            feed = feed_ref[span, :].astype(F32) + feed_got[span, :].astype(F32)
            down = down_ref[span, :].astype(F32) + down_got[span, :].astype(F32)
            out_ref[x, owner, :, :wide] = feed.astype(BF16)
            out_ref[x, owner, :, wide:] = down.astype(BF16)


def combine(feed, feed_got, down, down_got):
    model, wide = feed.shape
    parts, owners, steps = 4, 16, 4
    share = model // (parts * owners)
    total = wide + down.shape[1]

    def row(value):
        return pl.BlockSpec((model // steps, value.shape[1]), lambda i: (i, 0))

    result = pl.pallas_call(
        combine_kernel,
        out_shape=jax.ShapeDtypeStruct((parts, owners, share, total), BF16),
        grid=(steps,),
        in_specs=[row(feed), row(feed_got), row(down), row(down_got)],
        out_specs=pl.BlockSpec((parts, owners // steps, share, total), lambda i: (0, i, 0, 0)),
        compiler_params=pltpu.CompilerParams(vmem_limit_bytes=24 * 2**20),
        cost_estimate=pl.CostEstimate(flops=5_000_000, bytes_accessed=15_000_000, transcendentals=0),
        name="combine",
    )(feed, feed_got, down, down_got)
    return result.reshape(model, total)


def spill_kernel(sum_ref, gate_weight, lift_weight, gate_ref, lift_ref, down_ref, gain_ref):
    parts, owners, quarter, _ = sum_ref.shape
    hidden = down_ref.shape[0]
    width = parts * quarter
    for owner in range(owners):
        for x in range(parts):
            span = slice(x * quarter, (x + 1) * quarter)
            at = slice(owner * hidden, (owner + 1) * hidden)
            gate_ref[span, at] = sum_ref[x, owner, :, :hidden].astype(F32)
            lift_ref[span, at] = sum_ref[x, owner, :, SLOT : SLOT + hidden].astype(F32)
        block = sum_ref[:, owner, :, 2 * SLOT :].astype(F32).reshape(width, SLOT)
        down_ref[:, owner * width : (owner + 1) * width] = block.T[:hidden]
    gain_ref[...] = jnp.sum(
        gate_ref[...] * gate_weight[...].astype(F32) + lift_ref[...] * lift_weight[...].astype(F32),
        axis=1,
        keepdims=True,
    )


def spill(summed, gate_weight, lift_weight, hidden):
    parts, owners, quarter, _ = summed.shape
    shape = jax.ShapeDtypeStruct
    return pl.pallas_call(
        spill_kernel,
        out_shape=(shape((parts * quarter, owners * hidden), F32),) * 2
        + (shape((hidden, owners * parts * quarter), F32), shape((parts * quarter, 1), F32)),
        in_specs=kernel_specs(3)[1:],
        out_specs=tuple(kernel_specs(4)[1:]),
        compiler_params=pltpu.CompilerParams(vmem_limit_bytes=40 * 2**20),
        cost_estimate=pl.CostEstimate(flops=5_000_000, bytes_accessed=17_000_000, transcendentals=0),
        name="spill",
    )(summed, gate_weight, lift_weight)


def heads_kernel(fence, out_ref, out_got, up_ref, up_got, pack_ref):
    model = out_ref.shape[1]
    head = out_ref.shape[0] // 2
    share = head // 8
    owners = 16
    depth = up_ref.shape[0] // owners
    few = depth // 8
    for y in range(2):
        for part in range(8):
            at = part * 2 + y
            span = slice(y * head + part * share, y * head + (part + 1) * share)
            total = out_ref[span, :].astype(F32) + out_got[span, :].astype(F32)
            pack_ref[at, :share, :] = total.astype(BF16)
            cols = slice(y * head, (y + 1) * head)
            for pair in range(owners // 2):
                slabs = []
                for owner in (2 * pair, 2 * pair + 1):
                    rows_at = slice(owner * depth + part * few, owner * depth + (part + 1) * few)
                    slabs.append(
                        up_ref[rows_at, cols].astype(F32) + up_got[rows_at, cols].astype(F32)
                    )
                pack_ref[at, share:, pair * head : (pair + 1) * head] = jnp.concatenate(
                    slabs, axis=0
                ).astype(BF16)


def pack_heads(fence, out, out_got, up, up_got):
    head, model = out.shape[0] // 2, out.shape[1]
    return pl.pallas_call(
        heads_kernel,
        out_shape=jax.ShapeDtypeStruct((16, head // 8 + 16, model), BF16),
        in_specs=kernel_specs(4),
        out_specs=kernel_specs(1)[1],
        compiler_params=pltpu.CompilerParams(vmem_limit_bytes=24 * 2**20),
        cost_estimate=pl.CostEstimate(flops=2_000_000, bytes_accessed=9_500_000, transcendentals=0),
        name="pack_heads",
    )(fence, out, out_got, up, up_got)


def finish_kernel(
    last_ref,
    down_weight,
    key_weight,
    value_weight,
    up_weight,
    out_ref,
    up_ref,
    down_ref,
    key_ref,
    value_ref,
    first_ref,
    query_ref,
):
    parts, _, model = last_ref.shape
    out_rows, up_rows = out_ref.shape[0] // parts, up_ref.shape[0] // parts
    rows_each = down_ref.shape[0] // parts
    latent, head = down_ref.shape[1], key_ref.shape[1]
    for part in range(parts):
        out_ref[part * out_rows : (part + 1) * out_rows, :] = last_ref[part, :out_rows, :].astype(
            F32
        )
        up = last_ref[part, out_rows : out_rows + 2 * up_rows, :].astype(F32)
        span = slice(part * up_rows, (part + 1) * up_rows)
        up_ref[span, :model] = up[:up_rows]
        up_ref[span, model:] = up[up_rows:]
        first = last_ref[part, out_rows + 2 * up_rows :, :].astype(F32)
        span = slice(part * rows_each, (part + 1) * rows_each)
        down_ref[span, :] = first[:, :latent]
        key_ref[span, :] = first[:, latent : latent + head]
        value_ref[span, :] = first[:, latent + head : latent + 2 * head]
    total = None
    for grad, weight in ((down_ref, down_weight), (key_ref, key_weight), (value_ref, value_weight)):
        value = jnp.sum(grad[...] * weight[...].astype(F32), axis=1, keepdims=True)
        total = value if total is None else total + value
    first_ref[...] = total
    query_ref[...] = jnp.sum(up_ref[...] * up_weight[...].astype(F32), axis=1, keepdims=True)


def finish(last, down_weight, key_weight, value_weight, up_weight):
    parts, _, model = last.shape
    shape = jax.ShapeDtypeStruct
    width, depth, head = down_weight.shape[0], up_weight.shape[0], key_weight.shape[1]
    return pl.pallas_call(
        finish_kernel,
        out_shape=(
            shape((head, model), F32),
            shape(up_weight.shape, F32),
            shape(down_weight.shape, F32),
            shape(key_weight.shape, F32),
            shape(value_weight.shape, F32),
            shape((width, 1), F32),
            shape((depth, 1), F32),
        ),
        in_specs=kernel_specs(5)[1:],
        out_specs=tuple(kernel_specs(7)[1:]),
        compiler_params=pltpu.CompilerParams(vmem_limit_bytes=24 * 2**20),
        cost_estimate=pl.CostEstimate(flops=2_000_000, bytes_accessed=8_000_000, transcendentals=0),
        name="finish",
    )(last, down_weight, key_weight, value_weight, up_weight)


def feed_forward(normed, cotangent, own, sib, down):
    count, model = normed.shape
    tile, slots = 256, down.shape[0]
    row = pl.BlockSpec((tile, model), lambda i: (i, 0))
    slot_row = pl.BlockSpec((tile, slots), lambda i: (i, 0))

    def fixed(value):
        return pl.BlockSpec(value.shape, lambda i: (0,) * value.ndim)

    shape = jax.ShapeDtypeStruct
    return pl.pallas_call(
        feed_kernel,
        grid=(count // tile,),
        out_shape=(shape((count, slots), BF16),) * 3 + (shape((count, model), BF16),),
        in_specs=[row, row, fixed(own), fixed(sib), fixed(down)],
        out_specs=(slot_row,) * 3 + (row,),
        compiler_params=pltpu.CompilerParams(vmem_limit_bytes=52 * 2**20),
        cost_estimate=pl.CostEstimate(
            flops=19_000_000_000, bytes_accessed=32_000_000, transcendentals=800_000
        ),
        name="feed_forward",
    )(normed, cotangent, own, sib, down)


def attend_back(meta, branch, kv, up, proj, cosine, sine, place, begin, query, out, log, lane):
    blocks, _, rows_all = place.shape
    width, head = rows_all // 2, kv.shape[1] // 2
    shape = jax.ShapeDtypeStruct
    return pl.pallas_call(
        attend_back_kernel,
        out_shape=(
            shape(query.shape, BF16),
            shape((blocks, width, up.shape[0]), BF16),
            shape((2 * blocks, width, 2 * head), BF16),
            shape((2 * blocks, width, 2 * head), BF16),
            shape((2 * head, proj[0].shape[1]), BF16),
            shape((2 * head, proj[0].shape[1]), BF16),
            shape((up.shape[0], 2 * head), BF16),
            shape((up.shape[0], 2 * head), BF16),
        ),
        in_specs=kernel_specs(23),
        out_specs=tuple(kernel_specs(8)[1:]),
        scratch_shapes=[pltpu.VMEM(query.shape, BF16)]
        + [pltpu.VMEM((kv.shape[0], head), F32)] * 2,
        compiler_params=pltpu.CompilerParams(vmem_limit_bytes=48 * 2**20),
        cost_estimate=pl.CostEstimate(
            flops=24_000_000_000, bytes_accessed=20_000_000, transcendentals=3_400_000
        ),
        name="attend_back",
    )(meta, *branch, kv, up, *proj, cosine, sine, place, begin, query, out, log, *lane)


def shards(
    tokens,
    doc_lengths,
    first_gain,
    query_down,
    key_proj,
    value_proj,
    query_gain,
    query_up,
    out_proj,
    second_gain,
    gate_proj,
    up_proj,
    down_proj,
    cotangent,
):
    width, model = tokens.shape
    latent_width = query_down.shape[1]
    head = key_proj.shape[1]
    depth = query_up.shape[0]
    hidden_width = gate_proj.shape[1] // 16
    lane_width = latent_width + 2 * head

    v, x, y, z, c = (lax.axis_index(axis) for axis in AXES)

    weights = lax.all_gather(
        jnp.concatenate([query_down, key_proj, value_proj], axis=1), SEQ, axis=0, tiled=True
    )

    gain_rows = jnp.zeros((16, head), BF16)
    gain_rows = gain_rows.at[0, :width].set(first_gain).at[1, :width].set(second_gain)
    gain_rows = gain_rows.at[2, :depth].set(query_gain)
    heads = query_up.reshape(depth, 2, 8, head)
    quarter = width // 4
    feed_rows = [
        jnp.pad(
            lax.dynamic_slice_in_dim(weight, x * quarter, quarter, 0).reshape(
                quarter, 16, hidden_width
            ),
            ((0, 0), (0, 0), (0, SLOT - hidden_width)),
        )
        for weight in (gate_proj, up_proj)
    ]
    feed_rows = jnp.concatenate(feed_rows, axis=2)
    parts = [
        jnp.broadcast_to(heads[:, at].transpose(1, 0, 2)[None], (2, 8, depth, head)).reshape(
            16, depth, head
        )
        for at in range(2)
    ]
    parts = parts + [
        feed_rows[..., at * head : (at + 1) * head].transpose(1, 0, 2) for at in range(3)
    ]
    parts = parts + [jnp.broadcast_to(gain_rows[None], (16, 16, head))]
    swapped_weights = exchange(jnp.concatenate(parts, axis=1), SEQ)
    first_row = 2 * depth + 3 * quarter
    gain_one = swapped_weights[:, first_row, :width].reshape(1, model).astype(F32)
    gain_two = swapped_weights[:, first_row + 1, :width].reshape(1, model).astype(F32)
    gain_query = swapped_weights[:, first_row + 2, :depth].reshape(1, latent_width).astype(F32)
    up_pair = jnp.concatenate(
        [
            swapped_weights[:, at * depth : (at + 1) * depth].reshape(latent_width, head)
            for at in range(2)
        ],
        axis=1,
    )
    up_chip = jnp.concatenate([up_pair, sibling(up_pair)], axis=1)
    feed_parts = swapped_weights[:, 2 * depth : first_row].reshape(16 * 3 * quarter, head)

    lengths = doc_lengths[0]
    z_at = jnp.stack([z, (z + 2) % 4, (z + 1) % 4, (z + 3) % 4])
    blocks = (y * 4 + z_at) * 2 + c
    token_index = blocks[:, None] * width + jnp.arange(width, dtype=jnp.int32)[None, :]
    doc_start = layout(lengths, token_index.reshape(-1)).reshape(token_index.shape)
    cosine, sine = rope_tables((token_index - doc_start).reshape(-1), head)
    meta = jnp.concatenate([jnp.stack([y, c]), jnp.max(doc_start, axis=1), blocks])
    meta = meta.astype(jnp.int32)
    place_row = jnp.tile(token_index, (1, 2))[:, None, :]
    begin_row = jnp.tile(doc_start, (1, 2))[:, None, :]
    cos_own, sin_own = cosine[:width], sine[:width]

    tokens_float = tokens.astype(F32)
    inv_one = inverse_rms(tokens_float)
    with jax.named_scope("out_chip"):
        out_sib = sibling(out_proj)
    for piece in (up_chip, out_sib):
        gain_one = after(gain_one, piece)
    normed = (tokens_float * inv_one * gain_one).astype(BF16)
    first = dot(normed, weights)
    latent = first[:, :latent_width]
    inv_latent = inverse_rms(latent)
    latent_n = (latent * inv_latent * gain_query).astype(BF16)
    key_rot = rotate(first[:, latent_width : latent_width + head], cos_own, sin_own).astype(BF16)
    value_low = first[:, latent_width + head :].astype(BF16)

    kv = lax.all_gather(
        jnp.concatenate([key_rot, value_low], axis=1), SEQ, axis=0, tiled=True
    )
    with jax.named_scope("lane"):
        lane = ring_gather(latent_n)
    with jax.named_scope("out_chip"):
        out_across = turn(after(out_proj, first), "y", 1)
    lane = (lane[0], after(lane[1], out_across)) + lane[2:]
    query_rot = make_queries(lane, up_chip, cosine, sine, 4)
    with jax.named_scope("out_chip"):
        out_across_sib = sibling(after(out_across, query_rot))
    attended, log_total = attend(meta, query_rot, kv, place_row, begin_row)
    out_pieces = (out_proj, out_across, out_sib, out_across_sib)
    cot_all = lax.all_gather(after(after(cotangent, kv), query_rot), ("y", "z"), axis=0, tiled=True)
    attended_rows = attended.reshape(4 * width, 4 * head)
    mixed = project(meta, attended, out_pieces)
    with jax.named_scope("residual"):
        residual = tokens_float + ring_scatter(mixed)
    inv_two = inverse_rms(residual)
    normed_two = (residual * inv_two * gain_two).astype(BF16)

    normed_all = lax.all_gather(normed_two, ("y", "z"), axis=0, tiled=True)
    with jax.named_scope("feed_weights"):
        feed_ring = ring_gather(after(feed_parts, normed_two), "x")
        feed_own = jnp.zeros((3, 16, 4, quarter, head), BF16)
        for part, step, first_owner in zip(feed_ring, (0, 2, 2, 1, 3), (0, 0, 8, 0, 0)):
            part = part.reshape(-1, 3, quarter, head).transpose(1, 0, 2, 3)[:, :, None]
            feed_own = lax.dynamic_update_slice(
                feed_own, part, (0, first_owner, (x + step) % 4, 0, 0)
            )
        feed_own = feed_own.reshape(3, model, head)
        feed_sib = sibling(feed_own)
        down_own = jnp.pad(down_proj, ((0, SLOT - hidden_width), (0, 0)))
        down_chip = jnp.concatenate([down_own, sibling(after(down_own, kv))], axis=0)
    hidden, grad_own, grad_sib, back = feed_forward(
        normed_all, cot_all, feed_own, feed_sib, down_chip
    )
    grad_normed_two = lax.psum_scatter(back, ("y", "z"), scatter_dimension=0, tiled=True)
    grad_normed_two = grad_normed_two.astype(F32)

    with jax.named_scope("feed_grad"):
        feed_other = sibling(dot_tn(normed_all, grad_sib).astype(BF16))
        down_other = sibling(dot_tn(cot_all, hidden[:, SLOT:]).astype(BF16))
        feed_grad = dot_tn(normed_all, grad_own).astype(BF16)
        down_grad = dot_tn(cot_all, hidden[:, :SLOT]).astype(BF16)
    with jax.named_scope("feed_grad"):
        feed_grad = combine(feed_grad, feed_other, down_grad, down_other)
        feed_part = lax.psum_scatter(feed_grad, "x", scatter_dimension=0, tiled=True)
        fed = lax.optimization_barrier(dot(hidden, down_chip).astype(BF16))
    grad_normed_two = after(after(grad_normed_two, feed_grad), fed)
    grad_two = rms_back(residual, inv_two, gain_two, grad_normed_two)
    grad_residual = cotangent.astype(F32) + grad_two

    with jax.named_scope("branch"):
        branch = ring_gather(grad_residual.astype(BF16))
    with jax.named_scope("layer_out"):
        fed = fed.reshape(2, 4 * width, model)
        fed_own = lax.dynamic_index_in_dim(fed, y, 0, keepdims=False)
        fed_across = lax.dynamic_index_in_dim(fed, 1 - y, 0, keepdims=False)
        fed_across = turn(after(fed_across, branch[1]), "y", 1)
    grad_queries, latent_parts, kv_own, kv_sib, out_grad, out_grad_sib, up_grad, up_sib = attend_back(
        meta,
        branch,
        kv,
        up_chip,
        out_pieces,
        cosine,
        sine,
        place_row,
        begin_row,
        query_rot,
        attended,
        log_total,
        lane,
    )
    with jax.named_scope("feed_grad"):
        feed_part = feed_part.reshape(16, quarter, 3 * SLOT)
        swapped = exchange(feed_part[..., : 2 * SLOT], SEQ)
    with jax.named_scope("latent_grad"):
        grad_latent_n = ring_scatter(latent_parts)
    with jax.named_scope("heads_grad"):
        heads_parts = pack_heads(
            ((fed_across[0, 0] + grad_latent_n[0, 0] + swapped[0, 0, 0]) * 0).astype(jnp.int32).reshape(1),
            out_grad,
            sibling(out_grad_sib),
            up_grad,
            sibling(up_sib),
        )
        heads_got = exchange(heads_parts, ACROSS)
    with jax.named_scope("kv_grad"):
        kv_grad = kv_own.astype(F32) + sibling(kv_sib).astype(F32)
        kv_grad = after(kv_grad, heads_got).astype(BF16)
        kv_sum = total_of(exchange(kv_grad, ("y", "z")))
    grad_keys = rotate_back(kv_sum[:, :head], cos_own, sin_own).astype(BF16)
    grad_values = kv_sum[:, head:].astype(BF16)
    grad_latent = rms_back(latent, inv_latent, gain_query, grad_latent_n)
    grad_latent = grad_latent.astype(BF16)
    grad_first = jnp.concatenate([grad_latent, grad_keys, grad_values], axis=1)
    with jax.named_scope("first_lane"):
        first_lane = ring_gather(grad_first)
    with jax.named_scope("columns"):
        columns = pick_columns(normed, z + (kv_sum[0, 0] * 0).astype(jnp.int32), c)
        columns = (columns[0],) + tuple(
            turn(part, "z", -step) for part, step in zip(columns[1:], (2, 1, 3))
        )
    own_first, first_other = first_weights(columns, first_lane)
    own_first = own_first + sibling(first_other).astype(F32)
    with jax.named_scope("feed_grad"):
        feed_part = jnp.concatenate([swapped, feed_part[..., 2 * SLOT :]], axis=2)
        feed_across = after(turn(feed_part, "v", 1), kv_sum)
        feed_part = (feed_part.astype(F32) + feed_across.astype(F32)).astype(BF16)
        feed_sum = lax.all_gather(
            feed_part.reshape(16 * quarter, 3 * SLOT), "x", axis=0, tiled=True
        )
    with jax.named_scope("layer_out"):
        fed = fed_own.astype(F32) + after(fed_across.astype(F32), heads_parts)
        fed_part = lax.psum_scatter(fed.astype(BF16), "z", scatter_dimension=0, tiled=True)
        layer_out = (residual + fed_part.astype(F32)).astype(BF16)
    with jax.named_scope("heads_grad"):
        heads_part = total_of(heads_got).astype(BF16)
        out_part, up_part = heads_part[: head // 8], heads_part[head // 8 :]
        up_part = up_part.reshape(16, 8, head).transpose(1, 0, 2)
    with jax.named_scope("up_grad"):
        up_part = exchange(after(up_part, kv_sum).reshape(16, depth // 8, head), SEQ)
        up_part = up_part.reshape(2, 8, depth // 8, head).transpose(0, 2, 1, 3)
        up_part = up_part.reshape(-1, model)
    grad_normed = dot_nt(grad_latent, weights[:, :latent_width])
    grad_normed = grad_normed + dot_nt(grad_first[:, latent_width:], weights[:, latent_width:])
    grad_one = rms_back(tokens_float, inv_one, gain_one, grad_normed)
    input_grad = grad_residual + grad_one

    share = width // 8
    tail = own_first.reshape(2, 8, share, lane_width).transpose(1, 0, 2, 3)
    tail = total_of(exchange(tail.reshape(16, share, lane_width).astype(BF16), ACROSS))
    first_part = jnp.pad(tail.astype(BF16), ((0, 0), (0, model - lane_width)))
    last_sum = spread(jnp.concatenate([out_part, up_part, first_part], axis=0), DP)

    gate_sum, lift_sum, down_sum, second_gain_sum = spill(
        feed_sum.reshape(4, 16, quarter, 3 * SLOT), gate_proj, up_proj, hidden_width
    )
    out_sum, up_sum, down_first, key_sum, value_sum, first_gain_sum, query_gain_sum = finish(
        last_sum, query_down, after(key_proj, second_gain_sum), value_proj, query_up
    )
    first_gain_sum = first_gain_sum.reshape(-1) / first_gain.astype(F32)
    query_gain_sum = query_gain_sum.reshape(-1) / query_gain.astype(F32)
    second_gain_sum = second_gain_sum.reshape(-1) / second_gain.astype(F32)
    return (
        layer_out,
        input_grad,
        first_gain_sum,
        down_first,
        key_sum,
        value_sum,
        query_gain_sum,
        up_sum,
        out_sum,
        second_gain_sum,
        gate_sum,
        lift_sum,
        down_sum,
    )


def solution(mesh):
    fine = Mesh(mesh.devices.reshape(SIZES), AXES)
    split, groups = P(DP + SEQ, None), P(DP, None)
    matrix, vector = P(SEQ, None), P(SEQ)
    in_specs = (
        split,
        groups,
        vector,
        matrix,
        matrix,
        matrix,
        vector,
        matrix,
        matrix,
        vector,
        matrix,
        matrix,
        matrix,
        split,
    )
    out_specs = (
        split,
        split,
        vector,
        matrix,
        matrix,
        matrix,
        vector,
        matrix,
        matrix,
        vector,
        matrix,
        matrix,
        matrix,
    )
    return jax.shard_map(shards, mesh=fine, in_specs=in_specs, out_specs=out_specs, check_vma=False)
```

```python
import jax
import jax.numpy as jnp
from jax import lax
from jax.experimental import pallas as pl
from jax.experimental.pallas import tpu as pltpu
from jax.sharding import Mesh, PartitionSpec as P

NORM_EPSILON = 1e-05
F32 = jnp.float32
BF16 = jnp.bfloat16

AXES = ("v", "x", "y", "z", "c")
SIZES = (2, 4, 2, 4, 2)
DP, SEQ, ACROSS = ("v", "x"), ("y", "z", "c"), ("v", "x", "y")
SLOT = 384
KEY_CHUNK = 1024
BACK_CHUNK = 512


def turn(value, axis, step):
    size = SIZES[AXES.index(axis)]
    return lax.ppermute(value, axis, [(i, (i + step) % size) for i in range(size)])


def sibling(value):
    return turn(value, "c", 1)


def after(value, other):
    first = other[(0,) * other.ndim] if other.ndim else other
    return value + (first * 0).astype(value.dtype)


def rows(value, start, stop):
    return lax.slice_in_dim(value, start, stop, axis=0)


def exchange(parts, axes):
    return lax.all_to_all(parts, axes, 0, 0)


def spread(value, axes):
    count = 1
    for axis in axes:
        count *= SIZES[AXES.index(axis)]
    return exchange(jnp.broadcast_to(value[None], (count,) + value.shape), axes)


def total_of(parts):
    return jnp.sum(parts.astype(F32), axis=0)


def ring_gather(block, axis="z"):
    half = block.shape[0] // 2
    after_it, before_it = turn(block, axis, -1), turn(block, axis, 1)
    far_low = turn(rows(after_it, 0, half), axis, -1)
    far_high = turn(rows(before_it, half, 2 * half), axis, 1)
    return (block, far_low, far_high, after_it, before_it)


def ring_merge_kernel(part_ref, low_ref, high_ref, next_ref, back_ref):
    half = low_ref.shape[0]
    next_ref[half:, :] = part_ref[0, half:, :]
    next_ref[:half, :] = (part_ref[0, :half, :].astype(F32) + low_ref[...].astype(F32)).astype(BF16)
    back_ref[:half, :] = part_ref[1, :half, :]
    back_ref[half:, :] = (part_ref[1, half:, :].astype(F32) + high_ref[...].astype(F32)).astype(
        BF16
    )


def ring_scatter(parts, other=None):
    _, width, size = parts.shape
    half = width // 2
    got_low = turn(parts[1, :half], "z", 1)
    got_high = turn(parts[1, half:], "z", -1)
    if other is not None:
        got_low = after(got_low, other)
    half_spec = pl.BlockSpec((half, size), lambda i: (0, 0))
    full_spec = pl.BlockSpec((width, size), lambda i: (0, 0))
    to_next, to_back = pl.pallas_call(
        ring_merge_kernel,
        grid=(1,),
        out_shape=(jax.ShapeDtypeStruct((width, size), BF16),) * 2,
        in_specs=[pl.BlockSpec((2, width, size), lambda i: (1, 0, 0)), half_spec, half_spec],
        out_specs=(full_spec, full_spec),
        name="ring_merge",
    )(parts, got_low, got_high)
    return (
        parts[0].astype(F32)
        + turn(to_next, "z", 1).astype(F32)
        + turn(to_back, "z", -1).astype(F32)
    )


def inverse_rms(values):
    return lax.rsqrt(jnp.mean(values * values, axis=-1, keepdims=True) + NORM_EPSILON)


def rms_back(values, inv_root, gain_row, grad_normed):
    scaled = grad_normed * gain_row
    return inv_root * scaled - values * inv_root**3 * jnp.mean(
        scaled * values, axis=-1, keepdims=True
    )


def layout(lengths, token_index):
    doc_ends = jnp.cumsum(lengths)
    starts = doc_ends - lengths
    doc_id = jnp.sum((token_index[:, None] >= doc_ends[None, :]).astype(jnp.int32), axis=1)
    numbers = jnp.arange(lengths.shape[0], dtype=jnp.int32)
    doc_start = jnp.sum(jnp.where(doc_id[:, None] == numbers[None, :], starts[None, :], 0), axis=1)
    return doc_start


def rope_tables(position, head_width):
    half_width = head_width // 2
    frequency = 10000.0 ** (-(2.0 * jnp.arange(half_width, dtype=F32)) / head_width)
    angles = position.astype(F32)[:, None] * frequency[None, :]
    return (jnp.cos(angles), jnp.sin(angles))


def rotate(values, cosine, sine):
    half_width = cosine.shape[-1]
    low, high = values[..., :half_width], values[..., half_width:]
    return jnp.concatenate([low * cosine - high * sine, high * cosine + low * sine], axis=-1)


def rotate_back(grads, cosine, sine):
    return rotate(grads, cosine, -sine)


def dot(left, right):
    return jnp.dot(left, right, preferred_element_type=F32)


def dot_nt(left, right):
    return lax.dot_general(left, right, (((1,), (1,)), ((), ())), preferred_element_type=F32)


def dot_tn(left, right):
    return lax.dot_general(left, right, (((0,), (0,)), ((), ())), preferred_element_type=F32)


def masked(scores, first_key, place, begin):
    key = first_key + lax.broadcasted_iota(jnp.int32, scores.shape, 0)
    return jnp.where((key >= begin) & (key <= place), scores, -1e30)


def chunk_bounds(meta, block, width, size):
    number = meta[6 + block]
    count = ((number + 1) * width + size - 1) // size
    clear_from = jnp.minimum((meta[2 + block] + size - 1) // size, count)
    clear_to = jnp.maximum((number * width + 1) // size, clear_from)
    return clear_from, clear_to, count


def stack_lane(refs):
    return jnp.concatenate([ref[...] for ref in refs], axis=0)


def stack_heads(ref, block, head):
    count = ref.shape[2] // head
    return jnp.concatenate([ref[block, :, h * head : (h + 1) * head] for h in range(count)], axis=0)


def wide_row(ref, block, heads):
    return jnp.concatenate([ref[block]] * heads, axis=1)


def query_kernel(lane_a, lane_b, lane_c, lane_d, lane_e, up_ref, cos_ref, sin_ref, q_ref):
    blocks, width, size = q_ref.shape
    half = cos_ref.shape[1]
    head = 2 * half
    latent = stack_lane((lane_a, lane_b, lane_c, lane_d, lane_e))
    cosine, sine = cos_ref[...], sin_ref[...]
    for start in range(0, size, head):
        query = dot(latent, up_ref[:, start : start + head])
        low, high = query[:, :half], query[:, half:]
        turned = ((low * cosine - high * sine), (high * cosine + low * sine))
        for part, value in enumerate(turned):
            q_ref[:, :, start + part * half : start + (part + 1) * half] = (
                (value * head**-0.5).astype(BF16).reshape(blocks, width, half)
            )


def attend_kernel(meta, q_ref, kv_ref, place_ref, begin_ref, out_ref, log_ref):
    blocks, width, size = q_ref.shape
    head = kv_ref.shape[1] // 2
    heads = size // head
    rows_all = heads * width

    @pl.loop(0, blocks)
    def per_block(block):
        clear_from, clear_to, count = chunk_bounds(meta, block, width, KEY_CHUNK)
        place, begin = wide_row(place_ref, block, heads), wide_row(begin_ref, block, heads)
        query = stack_heads(q_ref, block, head)

        def chunk(step, carry, clear):
            top, total, mixed = carry
            start = pl.multiple_of(step * KEY_CHUNK, KEY_CHUNK)
            scores = dot_nt(kv_ref[pl.ds(start, KEY_CHUNK), :head], query)
            if not clear:
                scores = masked(scores, start, place, begin)
            new_top = jnp.maximum(top, jnp.max(scores, axis=0, keepdims=True))
            factor = jnp.exp(top - new_top)
            weights = jnp.exp(scores - new_top)
            total = total * factor + jnp.sum(weights, axis=0, keepdims=True)
            mixed = mixed * factor + dot_tn(
                kv_ref[pl.ds(start, KEY_CHUNK), head:], weights.astype(BF16)
            )
            return (new_top, total, mixed)

        carry = (
            jnp.full((1, rows_all), -1e30, F32),
            jnp.zeros((1, rows_all), F32),
            jnp.zeros((head, rows_all), F32),
        )
        carry = lax.fori_loop(0, clear_from, lambda s, w: chunk(s, w, False), carry)
        carry = lax.fori_loop(clear_from, clear_to, lambda s, w: chunk(s, w, True), carry)
        carry = lax.fori_loop(clear_to, count, lambda s, w: chunk(s, w, False), carry)
        top, total, mixed = carry
        result = (mixed / total).T.astype(BF16)
        for h in range(heads):
            out_ref[block, :, h * head : (h + 1) * head] = result[h * width : (h + 1) * width]
        log_ref[block] = top + jnp.log(total)


def attend_back_kernel(
    meta,
    branch_a,
    branch_b,
    branch_c,
    branch_d,
    branch_e,
    kv_ref,
    up_ref,
    proj_a,
    proj_b,
    proj_c,
    proj_d,
    cos_ref,
    sin_ref,
    place_ref,
    begin_ref,
    q_ref,
    out_ref,
    log_ref,
    lane_a,
    lane_b,
    lane_c,
    lane_d,
    lane_e,
    gq_ref,
    latent_ref,
    kv_own,
    kv_sib,
    out_own,
    out_sib,
    up_own,
    up_sib,
    grads,
    key_grad,
    value_grad,
):
    blocks, width, _ = q_ref.shape
    head = kv_ref.shape[1] // 2
    half = head // 2
    heads = q_ref.shape[2] // head
    branch = stack_lane((branch_a, branch_b, branch_c, branch_d, branch_e))
    y = meta[0]
    for at, (ref, yy) in enumerate(
        ((proj_a, y), (proj_b, 1 - y), (proj_c, y), (proj_d, 1 - y))
    ):
        first = pl.multiple_of((at // 2 * 2 + yy) * head, head)
        value = dot_nt(branch, ref[...])
        grads[:, :, pl.ds(first, head)] = value.astype(BF16).reshape(blocks, width, head)
    key_grad[...] = jnp.zeros_like(key_grad)
    value_grad[...] = jnp.zeros_like(value_grad)


    @pl.loop(0, blocks)
    def per_block(block):
        clear_from, clear_to, count = chunk_bounds(meta, block, width, BACK_CHUNK)
        place, begin = wide_row(place_ref, block, heads), wide_row(begin_ref, block, heads)
        token = pl.ds(pl.multiple_of(block * width, width), width)
        cosine, sine = cos_ref[token, :], sin_ref[token, :]
        query, grad, out = (stack_heads(ref, block, head) for ref in (q_ref, grads, out_ref))
        row_dot = jnp.sum((grad.astype(F32) * out.astype(F32)).T, axis=0, keepdims=True)
        log_total = log_ref[block]

        def chunk(step, acc, clear):
            start = pl.multiple_of(step * BACK_CHUNK, BACK_CHUNK)
            span = pl.ds(start, BACK_CHUNK)
            key_chunk = kv_ref[span, :head]
            scores = dot_nt(key_chunk, query)
            if not clear:
                scores = masked(scores, start, place, begin)
            probs = jnp.exp(scores - log_total)
            grad_probs = dot_nt(kv_ref[span, head:], grad)
            grad_scores = (probs * (grad_probs - row_dot)).astype(BF16)
            value_grad[span, :] += dot(probs.astype(BF16), grad)
            key_grad[span, :] += dot(grad_scores, query)
            return acc + dot_tn(grad_scores, key_chunk)

        acc = jnp.zeros((heads * width, head), F32)
        acc = lax.fori_loop(0, clear_from, lambda s, w: chunk(s, w, False), acc)
        acc = lax.fori_loop(clear_from, clear_to, lambda s, w: chunk(s, w, True), acc)
        acc = lax.fori_loop(clear_to, count, lambda s, w: chunk(s, w, False), acc)
        acc = acc * (head**-0.5)
        for h in range(heads):
            value = acc[h * width : (h + 1) * width]
            low, high = value[:, :half], value[:, half:]
            start = h * head
            gq_ref[block, :, start : start + half] = (low * cosine + high * sine).astype(BF16)
            gq_ref[block, :, start + half : start + head] = (high * cosine - low * sine).astype(BF16)

    grad_query = gq_ref[...].reshape(blocks * width, heads * head)
    size = latent_ref.shape[2]
    piece = 256
    for start in range(0, size, piece):
        value = dot_nt(grad_query, up_ref[start : start + piece, :])
        for slot in range(blocks):
            block = value[slot * width : (slot + 1) * width].astype(BF16)
            latent_ref[(meta[6 + slot] // 2) % 4, :, start : start + piece] = block
    mixed = out_ref[...].reshape(blocks * width, heads * head)
    latent = stack_lane((lane_a, lane_b, lane_c, lane_d, lane_e))
    for h in range(heads):
        span = slice(h * head, (h + 1) * head)
        at = slice((h % 2) * head, (h % 2 + 1) * head)
        target = (out_own, out_sib)[h // 2]
        target[at, :] = dot_tn(mixed[:, span], branch).astype(BF16)
        target = (up_own, up_sib)[h // 2]
        target[:, at] = dot_tn(latent, grad_query[:, span]).astype(BF16)
    c = meta[1]
    for chip in range(2 * blocks):
        for target, cc in ((kv_own, c), (kv_sib, 1 - c)):
            span = pl.ds(pl.multiple_of((chip * 2 + cc) * width, width), width)
            target[chip, :, :head] = key_grad[span, :].astype(BF16)
            target[chip, :, head:] = value_grad[span, :].astype(BF16)


def kernel_specs(count):
    smem = pl.BlockSpec(memory_space=pltpu.SMEM)
    vmem = pl.BlockSpec(memory_space=pltpu.VMEM)
    return [smem] + [vmem] * count


def column_kernel(meta, normed_ref, *targets):
    width = targets[0].shape[0]
    z, c = meta[0], meta[1]
    for step, target in zip((0, 2, 1, 3), targets):
        place = (z + 4 - step) % 4
        for at, (cc, y) in enumerate(((c, 0), (c, 1), (1 - c, 0), (1 - c, 1))):
            start = pl.multiple_of(((y * 4 + place) * 2 + cc) * width, width)
            target[:, at * width : (at + 1) * width] = normed_ref[:, pl.ds(start, width)]


def first_kernel(col_a, col_b, col_c, col_d, g_a, g_b, g_c, g_d, g_e, own_ref, other_ref):
    columns = stack_lane((col_a, col_b, col_c, col_d))
    grads = stack_lane((g_a, g_b, g_c, g_d, g_e))
    half = own_ref.shape[0]
    own_ref[...] = dot_tn(columns[:, :half], grads)
    other_ref[...] = dot_tn(columns[:, half:], grads).astype(BF16)


def first_weights(columns, lane):
    half, size = columns[0].shape[1] // 2, lane[0].shape[1]
    return pl.pallas_call(
        first_kernel,
        out_shape=(
            jax.ShapeDtypeStruct((half, size), F32),
            jax.ShapeDtypeStruct((half, size), BF16),
        ),
        in_specs=kernel_specs(9)[1:],
        out_specs=tuple(kernel_specs(2)[1:]),
        compiler_params=pltpu.CompilerParams(vmem_limit_bytes=16 * 2**20),
        cost_estimate=pl.CostEstimate(
            flops=800_000_000, bytes_accessed=5_000_000, transcendentals=0
        ),
        name="first_weights",
    )(*columns, *lane)


def pick_columns(normed, z, c):
    width = normed.shape[0]
    return pl.pallas_call(
        column_kernel,
        out_shape=(jax.ShapeDtypeStruct((width, 4 * width), BF16),) * 4,
        in_specs=kernel_specs(1),
        out_specs=tuple(kernel_specs(4)[1:]),
        name="pick_columns",
    )(jnp.stack([z, c]).astype(jnp.int32), normed)


def make_queries(lane, up, cosine, sine, blocks):
    width = lane[0].shape[0]
    return pl.pallas_call(
        query_kernel,
        out_shape=jax.ShapeDtypeStruct((blocks, width, up.shape[1]), BF16),
        in_specs=kernel_specs(8)[1:],
        out_specs=kernel_specs(1)[1],
        compiler_params=pltpu.CompilerParams(vmem_limit_bytes=24 * 2**20),
        cost_estimate=pl.CostEstimate(
            flops=1_100_000_000, bytes_accessed=5_000_000, transcendentals=0
        ),
        name="make_queries",
    )(*lane, up, cosine, sine)


def attend(meta, query, kv, place, begin):
    blocks, width, size = query.shape
    head = kv.shape[1] // 2
    shape = jax.ShapeDtypeStruct
    return pl.pallas_call(
        attend_kernel,
        out_shape=(
            shape(query.shape, BF16),
            shape((blocks, 1, size // head * width), F32),
        ),
        in_specs=kernel_specs(4),
        out_specs=tuple(kernel_specs(2)[1:]),
        compiler_params=pltpu.CompilerParams(vmem_limit_bytes=32 * 2**20),
        cost_estimate=pl.CostEstimate(
            flops=20_000_000_000, bytes_accessed=5_000_000, transcendentals=3_400_000
        ),
        name="attend",
    )(meta, query, kv, place, begin)


def project_kernel(meta, mixed_ref, own_ref, across_ref, sib_ref, across_sib_ref, part_ref):
    blocks, width, model = part_ref.shape
    head = own_ref.shape[0]
    y = meta[0]
    piece = 512
    for start in range(0, model, piece):
        total = None
        for at, (ref, yy) in enumerate(
            ((own_ref, y), (across_ref, 1 - y), (sib_ref, y), (across_sib_ref, 1 - y))
        ):
            first = pl.multiple_of((at // 2 * 2 + yy) * head, head)
            left = mixed_ref[:, :, pl.ds(first, head)].reshape(blocks * width, head)
            value = dot(left, ref[:, start : start + piece])
            total = value if total is None else total + value
        part_ref[:, :, start : start + piece] = total.astype(BF16).reshape(blocks, width, piece)


def project(meta, mixed, pieces):
    blocks, width, _ = mixed.shape
    model = pieces[0].shape[1]
    return pl.pallas_call(
        project_kernel,
        out_shape=jax.ShapeDtypeStruct((blocks, width, model), BF16),
        in_specs=kernel_specs(5),
        out_specs=kernel_specs(1)[1],
        compiler_params=pltpu.CompilerParams(vmem_limit_bytes=24 * 2**20),
        cost_estimate=pl.CostEstimate(
            flops=2_200_000_000, bytes_accessed=7_500_000, transcendentals=0
        ),
        name="project",
    )(meta, mixed, *pieces)


def feed_kernel(n_ref, cot_ref, own_ref, sib_ref, down_ref, hid_ref, go_ref, gs_ref, back_ref):
    slot = down_ref.shape[0] // 2
    blocks, _, size = own_ref.shape
    normed = n_ref[...]
    grad_hidden = dot_nt(cot_ref[...], down_ref[...])
    back = None
    for at, (weight, grad_ref) in enumerate(((own_ref, go_ref), (sib_ref, gs_ref))):
        span = slice(at * slot, (at + 1) * slot)
        both = jnp.concatenate([dot(normed, weight[i]) for i in range(blocks)], axis=1)
        gate, lift = both[:, :slot], both[:, slot:]
        grad = grad_hidden[:, span]
        sigmoid = jax.nn.sigmoid(gate)
        active = gate * sigmoid
        hid_ref[:, span] = (active * lift).astype(BF16)
        grad_ref[:, :slot] = (grad * lift * sigmoid * (1.0 + gate * (1.0 - sigmoid))).astype(BF16)
        grad_ref[:, slot:] = (grad * active).astype(BF16)
        for i in range(blocks):
            part = dot_nt(grad_ref[:, i * size : (i + 1) * size], weight[i])
            back = part if back is None else back + part
    back_ref[...] = back.astype(BF16)


def combine_kernel(feed_ref, feed_got, down_ref, down_got, out_ref):
    parts, owners, quarter, _ = out_ref.shape
    wide = feed_ref.shape[1]
    for owner in range(owners):
        for x in range(parts):
            span = slice((owner * parts + x) * quarter, (owner * parts + x + 1) * quarter)
            feed = feed_ref[span, :].astype(F32) + feed_got[span, :].astype(F32)
            down = down_ref[span, :].astype(F32) + down_got[span, :].astype(F32)
            out_ref[x, owner, :, :wide] = feed.astype(BF16)
            out_ref[x, owner, :, wide:] = down.astype(BF16)


def combine(feed, feed_got, down, down_got):
    model, wide = feed.shape
    parts, owners, steps = 4, 16, 4
    share = model // (parts * owners)
    total = wide + down.shape[1]

    def row(value):
        return pl.BlockSpec((model // steps, value.shape[1]), lambda i: (i, 0))

    result = pl.pallas_call(
        combine_kernel,
        out_shape=jax.ShapeDtypeStruct((parts, owners, share, total), BF16),
        grid=(steps,),
        in_specs=[row(feed), row(feed_got), row(down), row(down_got)],
        out_specs=pl.BlockSpec((parts, owners // steps, share, total), lambda i: (0, i, 0, 0)),
        compiler_params=pltpu.CompilerParams(vmem_limit_bytes=24 * 2**20),
        cost_estimate=pl.CostEstimate(flops=5_000_000, bytes_accessed=15_000_000, transcendentals=0),
        name="combine",
    )(feed, feed_got, down, down_got)
    return result.reshape(model, total)


def spill_kernel(sum_ref, gate_weight, lift_weight, gate_ref, lift_ref, down_ref, gain_ref):
    parts, owners, quarter, _ = sum_ref.shape
    hidden = down_ref.shape[0]
    width = parts * quarter
    for owner in range(owners):
        for x in range(parts):
            span = slice(x * quarter, (x + 1) * quarter)
            at = slice(owner * hidden, (owner + 1) * hidden)
            gate_ref[span, at] = sum_ref[x, owner, :, :hidden].astype(F32)
            lift_ref[span, at] = sum_ref[x, owner, :, SLOT : SLOT + hidden].astype(F32)
        block = sum_ref[:, owner, :, 2 * SLOT :].astype(F32).reshape(width, SLOT)
        down_ref[:, owner * width : (owner + 1) * width] = block.T[:hidden]
    gain_ref[...] = jnp.sum(
        gate_ref[...] * gate_weight[...].astype(F32) + lift_ref[...] * lift_weight[...].astype(F32),
        axis=1,
        keepdims=True,
    )


def spill(summed, gate_weight, lift_weight, hidden):
    parts, owners, quarter, _ = summed.shape
    shape = jax.ShapeDtypeStruct
    return pl.pallas_call(
        spill_kernel,
        out_shape=(shape((parts * quarter, owners * hidden), F32),) * 2
        + (shape((hidden, owners * parts * quarter), F32), shape((parts * quarter, 1), F32)),
        in_specs=kernel_specs(3)[1:],
        out_specs=tuple(kernel_specs(4)[1:]),
        compiler_params=pltpu.CompilerParams(vmem_limit_bytes=40 * 2**20),
        cost_estimate=pl.CostEstimate(flops=5_000_000, bytes_accessed=17_000_000, transcendentals=0),
        name="spill",
    )(summed, gate_weight, lift_weight)


def heads_kernel(fence, out_ref, out_got, up_ref, up_got, pack_ref):
    model = out_ref.shape[1]
    head = out_ref.shape[0] // 2
    share = head // 8
    owners = 16
    depth = up_ref.shape[0] // owners
    few = depth // 8
    for y in range(2):
        for part in range(8):
            at = part * 2 + y
            span = slice(y * head + part * share, y * head + (part + 1) * share)
            total = out_ref[span, :].astype(F32) + out_got[span, :].astype(F32)
            pack_ref[at, :share, :] = total.astype(BF16)
            cols = slice(y * head, (y + 1) * head)
            for pair in range(owners // 2):
                slabs = []
                for owner in (2 * pair, 2 * pair + 1):
                    rows_at = slice(owner * depth + part * few, owner * depth + (part + 1) * few)
                    slabs.append(
                        up_ref[rows_at, cols].astype(F32) + up_got[rows_at, cols].astype(F32)
                    )
                pack_ref[at, share:, pair * head : (pair + 1) * head] = jnp.concatenate(
                    slabs, axis=0
                ).astype(BF16)


def pack_heads(fence, out, out_got, up, up_got):
    head, model = out.shape[0] // 2, out.shape[1]
    return pl.pallas_call(
        heads_kernel,
        out_shape=jax.ShapeDtypeStruct((16, head // 8 + 16, model), BF16),
        in_specs=kernel_specs(4),
        out_specs=kernel_specs(1)[1],
        compiler_params=pltpu.CompilerParams(vmem_limit_bytes=24 * 2**20),
        cost_estimate=pl.CostEstimate(flops=2_000_000, bytes_accessed=9_500_000, transcendentals=0),
        name="pack_heads",
    )(fence, out, out_got, up, up_got)


def finish_kernel(
    last_ref,
    down_weight,
    key_weight,
    value_weight,
    up_weight,
    out_ref,
    up_ref,
    down_ref,
    key_ref,
    value_ref,
    first_ref,
    query_ref,
):
    parts, _, model = last_ref.shape
    out_rows, up_rows = out_ref.shape[0] // parts, up_ref.shape[0] // parts
    rows_each = down_ref.shape[0] // parts
    latent, head = down_ref.shape[1], key_ref.shape[1]
    for part in range(parts):
        out_ref[part * out_rows : (part + 1) * out_rows, :] = last_ref[part, :out_rows, :].astype(
            F32
        )
        up = last_ref[part, out_rows : out_rows + 2 * up_rows, :].astype(F32)
        span = slice(part * up_rows, (part + 1) * up_rows)
        up_ref[span, :model] = up[:up_rows]
        up_ref[span, model:] = up[up_rows:]
        first = last_ref[part, out_rows + 2 * up_rows :, :].astype(F32)
        span = slice(part * rows_each, (part + 1) * rows_each)
        down_ref[span, :] = first[:, :latent]
        key_ref[span, :] = first[:, latent : latent + head]
        value_ref[span, :] = first[:, latent + head : latent + 2 * head]
    total = None
    for grad, weight in ((down_ref, down_weight), (key_ref, key_weight), (value_ref, value_weight)):
        value = jnp.sum(grad[...] * weight[...].astype(F32), axis=1, keepdims=True)
        total = value if total is None else total + value
    first_ref[...] = total
    query_ref[...] = jnp.sum(up_ref[...] * up_weight[...].astype(F32), axis=1, keepdims=True)


def finish(last, down_weight, key_weight, value_weight, up_weight):
    parts, _, model = last.shape
    shape = jax.ShapeDtypeStruct
    width, depth, head = down_weight.shape[0], up_weight.shape[0], key_weight.shape[1]
    return pl.pallas_call(
        finish_kernel,
        out_shape=(
            shape((head, model), F32),
            shape(up_weight.shape, F32),
            shape(down_weight.shape, F32),
            shape(key_weight.shape, F32),
            shape(value_weight.shape, F32),
            shape((width, 1), F32),
            shape((depth, 1), F32),
        ),
        in_specs=kernel_specs(5)[1:],
        out_specs=tuple(kernel_specs(7)[1:]),
        compiler_params=pltpu.CompilerParams(vmem_limit_bytes=24 * 2**20),
        cost_estimate=pl.CostEstimate(flops=2_000_000, bytes_accessed=8_000_000, transcendentals=0),
        name="finish",
    )(last, down_weight, key_weight, value_weight, up_weight)


def feed_forward(normed, cotangent, own, sib, down):
    count, model = normed.shape
    tile, slots = 256, down.shape[0]
    row = pl.BlockSpec((tile, model), lambda i: (i, 0))
    slot_row = pl.BlockSpec((tile, slots), lambda i: (i, 0))

    def fixed(value):
        return pl.BlockSpec(value.shape, lambda i: (0,) * value.ndim)

    shape = jax.ShapeDtypeStruct
    return pl.pallas_call(
        feed_kernel,
        grid=(count // tile,),
        out_shape=(shape((count, slots), BF16),) * 3 + (shape((count, model), BF16),),
        in_specs=[row, row, fixed(own), fixed(sib), fixed(down)],
        out_specs=(slot_row,) * 3 + (row,),
        compiler_params=pltpu.CompilerParams(vmem_limit_bytes=52 * 2**20),
        cost_estimate=pl.CostEstimate(
            flops=19_000_000_000, bytes_accessed=32_000_000, transcendentals=800_000
        ),
        name="feed_forward",
    )(normed, cotangent, own, sib, down)


def attend_back(meta, branch, kv, up, proj, cosine, sine, place, begin, query, out, log, lane):
    blocks, _, width = place.shape
    head = kv.shape[1] // 2
    shape = jax.ShapeDtypeStruct
    return pl.pallas_call(
        attend_back_kernel,
        out_shape=(
            shape(query.shape, BF16),
            shape((blocks, width, up.shape[0]), BF16),
            shape((2 * blocks, width, 2 * head), BF16),
            shape((2 * blocks, width, 2 * head), BF16),
            shape((2 * head, proj[0].shape[1]), BF16),
            shape((2 * head, proj[0].shape[1]), BF16),
            shape((up.shape[0], 2 * head), BF16),
            shape((up.shape[0], 2 * head), BF16),
        ),
        in_specs=kernel_specs(23),
        out_specs=tuple(kernel_specs(8)[1:]),
        scratch_shapes=[pltpu.VMEM(query.shape, BF16)]
        + [pltpu.VMEM((kv.shape[0], head), F32)] * 2,
        compiler_params=pltpu.CompilerParams(vmem_limit_bytes=48 * 2**20),
        cost_estimate=pl.CostEstimate(
            flops=24_000_000_000, bytes_accessed=20_000_000, transcendentals=3_400_000
        ),
        name="attend_back",
    )(meta, *branch, kv, up, *proj, cosine, sine, place, begin, query, out, log, *lane)


def shards(
    tokens,
    doc_lengths,
    first_gain,
    query_down,
    key_proj,
    value_proj,
    query_gain,
    query_up,
    out_proj,
    second_gain,
    gate_proj,
    up_proj,
    down_proj,
    cotangent,
):
    width, model = tokens.shape
    latent_width = query_down.shape[1]
    head = key_proj.shape[1]
    depth = query_up.shape[0]
    hidden_width = gate_proj.shape[1] // 16
    lane_width = latent_width + 2 * head

    v, x, y, z, c = (lax.axis_index(axis) for axis in AXES)

    weights = lax.all_gather(
        jnp.concatenate([query_down, key_proj, value_proj], axis=1), SEQ, axis=0, tiled=True
    )

    gain_rows = jnp.zeros((16, head), BF16)
    gain_rows = gain_rows.at[0, :width].set(first_gain).at[1, :width].set(second_gain)
    gain_rows = gain_rows.at[2, :depth].set(query_gain)
    heads = query_up.reshape(depth, 2, 8, head)
    quarter = width // 4
    feed_rows = [
        jnp.pad(
            lax.dynamic_slice_in_dim(weight, x * quarter, quarter, 0).reshape(
                quarter, 16, hidden_width
            ),
            ((0, 0), (0, 0), (0, SLOT - hidden_width)),
        )
        for weight in (gate_proj, up_proj)
    ]
    feed_rows = jnp.concatenate(feed_rows, axis=2)
    parts = [
        jnp.broadcast_to(heads[:, at].transpose(1, 0, 2)[None], (2, 8, depth, head)).reshape(
            16, depth, head
        )
        for at in range(2)
    ]
    parts = parts + [
        feed_rows[..., at * head : (at + 1) * head].transpose(1, 0, 2) for at in range(3)
    ]
    parts = parts + [jnp.broadcast_to(gain_rows[None], (16, 16, head))]
    swapped_weights = exchange(jnp.concatenate(parts, axis=1), SEQ)
    first_row = 2 * depth + 3 * quarter
    gain_one = swapped_weights[:, first_row, :width].reshape(1, model).astype(F32)
    gain_two = swapped_weights[:, first_row + 1, :width].reshape(1, model).astype(F32)
    gain_query = swapped_weights[:, first_row + 2, :depth].reshape(1, latent_width).astype(F32)
    up_pair = jnp.concatenate(
        [
            swapped_weights[:, at * depth : (at + 1) * depth].reshape(latent_width, head)
            for at in range(2)
        ],
        axis=1,
    )
    up_chip = jnp.concatenate([up_pair, sibling(up_pair)], axis=1)
    feed_parts = swapped_weights[:, 2 * depth : first_row].reshape(16 * 3 * quarter, head)

    lengths = doc_lengths[0]
    z_at = jnp.stack([z, (z + 2) % 4, (z + 1) % 4, (z + 3) % 4])
    blocks = (y * 4 + z_at) * 2 + c
    token_index = blocks[:, None] * width + jnp.arange(width, dtype=jnp.int32)[None, :]
    doc_start = layout(lengths, token_index.reshape(-1)).reshape(token_index.shape)
    cosine, sine = rope_tables((token_index - doc_start).reshape(-1), head)
    meta = jnp.concatenate([jnp.stack([y, c]), jnp.max(doc_start, axis=1), blocks])
    meta = meta.astype(jnp.int32)
    place_row = token_index[:, None, :]
    begin_row = doc_start[:, None, :]
    cos_own, sin_own = cosine[:width], sine[:width]

    tokens_float = tokens.astype(F32)
    inv_one = inverse_rms(tokens_float)
    with jax.named_scope("out_chip"):
        out_sib = sibling(out_proj)
    for piece in (up_chip, out_sib):
        gain_one = after(gain_one, piece)
    normed = (tokens_float * inv_one * gain_one).astype(BF16)
    first = dot(normed, weights)
    latent = first[:, :latent_width]
    inv_latent = inverse_rms(latent)
    latent_n = (latent * inv_latent * gain_query).astype(BF16)
    key_rot = rotate(first[:, latent_width : latent_width + head], cos_own, sin_own).astype(BF16)
    value_low = first[:, latent_width + head :].astype(BF16)

    kv = lax.all_gather(
        jnp.concatenate([key_rot, value_low], axis=1), SEQ, axis=0, tiled=True
    )
    with jax.named_scope("lane"):
        lane = ring_gather(latent_n)
    with jax.named_scope("out_chip"):
        out_across = turn(after(out_proj, first), "y", 1)
    lane = (lane[0], after(lane[1], out_across)) + lane[2:]
    query_rot = make_queries(lane, up_chip, cosine, sine, 4)
    with jax.named_scope("out_chip"):
        out_across_sib = sibling(after(out_across, query_rot))
    attended, log_total = attend(meta, query_rot, kv, place_row, begin_row)
    out_pieces = (out_proj, out_across, out_sib, out_across_sib)
    cot_all = lax.all_gather(after(cotangent, first), ("y", "z"), axis=0, tiled=True)
    attended_rows = attended.reshape(4 * width, 4 * head)
    mixed = project(meta, attended, out_pieces)
    with jax.named_scope("residual"):
        residual = tokens_float + ring_scatter(mixed)
    inv_two = inverse_rms(residual)
    normed_two = (residual * inv_two * gain_two).astype(BF16)

    normed_all = lax.all_gather(normed_two, ("y", "z"), axis=0, tiled=True)
    with jax.named_scope("feed_weights"):
        feed_ring = ring_gather(after(feed_parts, normed_two), "x")
        feed_own = jnp.zeros((3, 16, 4, quarter, head), BF16)
        for part, step, first_owner in zip(feed_ring, (0, 2, 2, 1, 3), (0, 0, 8, 0, 0)):
            part = part.reshape(-1, 3, quarter, head).transpose(1, 0, 2, 3)[:, :, None]
            feed_own = lax.dynamic_update_slice(
                feed_own, part, (0, first_owner, (x + step) % 4, 0, 0)
            )
        feed_own = feed_own.reshape(3, model, head)
        feed_sib = sibling(feed_own)
        down_own = jnp.pad(down_proj, ((0, SLOT - hidden_width), (0, 0)))
        down_chip = jnp.concatenate([down_own, sibling(after(down_own, kv))], axis=0)
    hidden, grad_own, grad_sib, back = feed_forward(
        normed_all, cot_all, feed_own, feed_sib, down_chip
    )
    grad_normed_two = lax.psum_scatter(back, ("y", "z"), scatter_dimension=0, tiled=True)
    grad_normed_two = grad_normed_two.astype(F32)

    with jax.named_scope("feed_grad"):
        feed_other = sibling(dot_tn(normed_all, grad_sib).astype(BF16))
        down_other = sibling(dot_tn(cot_all, hidden[:, SLOT:]).astype(BF16))
        feed_grad = dot_tn(normed_all, grad_own).astype(BF16)
        down_grad = dot_tn(cot_all, hidden[:, :SLOT]).astype(BF16)
    with jax.named_scope("feed_grad"):
        feed_grad = combine(feed_grad, feed_other, down_grad, down_other)
        feed_part = lax.psum_scatter(feed_grad, "x", scatter_dimension=0, tiled=True)
        fed = lax.optimization_barrier(dot(hidden, down_chip).astype(BF16))
    grad_normed_two = after(after(grad_normed_two, feed_grad), fed)
    grad_two = rms_back(residual, inv_two, gain_two, grad_normed_two)
    grad_residual = cotangent.astype(F32) + grad_two

    with jax.named_scope("branch"):
        branch = ring_gather(grad_residual.astype(BF16))
    with jax.named_scope("layer_out"):
        fed = fed.reshape(2, 4 * width, model)
        fed_own = lax.dynamic_index_in_dim(fed, y, 0, keepdims=False)
        fed_across = lax.dynamic_index_in_dim(fed, 1 - y, 0, keepdims=False)
        fed_across = turn(after(fed_across, grad_residual), "y", 1)
    grad_queries, latent_parts, kv_own, kv_sib, out_grad, out_grad_sib, up_grad, up_sib = attend_back(
        meta,
        branch,
        kv,
        up_chip,
        out_pieces,
        cosine,
        sine,
        place_row,
        begin_row,
        query_rot,
        attended,
        log_total,
        lane,
    )
    with jax.named_scope("kv_grad"):
        kv_grad = kv_own.astype(F32) + sibling(kv_sib).astype(F32)
        kv_grad = after(kv_grad, feed_part[0, 0] + fed_across[0, 0]).astype(BF16)
        kv_sum = total_of(exchange(kv_grad, ("y", "z")))
    with jax.named_scope("feed_grad"):
        feed_part = after(feed_part, grad_queries)
        feed_across = turn(feed_part, "v", 1)
        feed_part = (feed_part.astype(F32) + feed_across.astype(F32)).astype(BF16)
        feed_part = feed_part.reshape(16, quarter, 3 * SLOT)
        v_sum = feed_part
        swapped = exchange(after(feed_part[..., : 2 * SLOT], kv_sum), SEQ)
        feed_part = jnp.concatenate([swapped, feed_part[..., 2 * SLOT :]], axis=2)
        feed_sum = lax.all_gather(
            feed_part.reshape(16 * quarter, 3 * SLOT), "x", axis=0, tiled=True
        )
    with jax.named_scope("latent_grad"):
        latent_parts = latent_parts.reshape(4 * width, latent_width)
        grad_latent_n = lax.psum_scatter(latent_parts, "z", scatter_dimension=0, tiled=True)
        grad_latent_n = grad_latent_n.astype(F32)
    with jax.named_scope("heads_grad"):
        heads_parts = pack_heads(
            ((swapped[0, 0, 0] + grad_latent_n[0, 0]) * 0).astype(jnp.int32).reshape(1),
            out_grad,
            sibling(out_grad_sib),
            up_grad,
            sibling(up_sib),
        )
        heads_got = exchange(heads_parts, ACROSS)
    grad_keys = rotate_back(kv_sum[:, :head], cos_own, sin_own).astype(BF16)
    grad_values = after(kv_sum[:, head:], v_sum).astype(BF16)
    grad_latent = rms_back(latent, inv_latent, gain_query, grad_latent_n)
    grad_latent = grad_latent.astype(BF16)
    grad_first = jnp.concatenate([grad_latent, grad_keys, grad_values], axis=1)
    with jax.named_scope("first_lane"):
        first_lane = ring_gather(grad_first)
    with jax.named_scope("columns"):
        columns = pick_columns(normed, z + (kv_sum[0, 0] * 0).astype(jnp.int32), c)
        columns = (columns[0],) + tuple(
            turn(part, "z", -step) for part, step in zip(columns[1:], (2, 1, 3))
        )
    own_first, first_other = first_weights(columns, first_lane)
    own_first = own_first + sibling(first_other).astype(F32)
    with jax.named_scope("heads_grad"):
        heads_part = total_of(heads_got).astype(BF16)
        out_part, up_part = heads_part[: head // 8], heads_part[head // 8 :]
        up_part = up_part.reshape(16, 8, head).transpose(1, 0, 2)
    grad_normed = dot_nt(grad_latent, weights[:, :latent_width])
    grad_normed = grad_normed + dot_nt(grad_first[:, latent_width:], weights[:, latent_width:])
    grad_one = rms_back(tokens_float, inv_one, gain_one, grad_normed)
    input_grad = grad_residual + grad_one

    share = width // 8
    tail = after(after(own_first, input_grad), heads_got).reshape(2, 8, share, lane_width).transpose(1, 0, 2, 3)
    tail = total_of(exchange(tail.reshape(16, share, lane_width).astype(BF16), ACROSS))
    with jax.named_scope("up_grad"):
        up_part = exchange(after(up_part, tail).reshape(16, depth // 8, head), SEQ)
        up_part = up_part.reshape(2, 8, depth // 8, head).transpose(0, 2, 1, 3)
        up_part = up_part.reshape(-1, model)
    with jax.named_scope("layer_out"):
        fed = fed_own.astype(F32) + after(fed_across.astype(F32), up_part)
        fed_part = lax.psum_scatter(fed.astype(BF16), "z", scatter_dimension=0, tiled=True)
        layer_out = (residual + fed_part.astype(F32)).astype(BF16)
    with jax.named_scope("heads_sum"):
        first_part = jnp.pad(tail.astype(BF16), ((0, 0), (0, model - lane_width)))
        last_sum = spread(jnp.concatenate([out_part, up_part, first_part], axis=0), DP)
    gate_sum, lift_sum, down_sum, second_gain_sum = spill(
        feed_sum.reshape(4, 16, quarter, 3 * SLOT), gate_proj, up_proj, hidden_width
    )
    out_sum, up_sum, down_first, key_sum, value_sum, first_gain_sum, query_gain_sum = finish(
        last_sum, query_down, after(key_proj, second_gain_sum), value_proj, query_up
    )
    first_gain_sum = first_gain_sum.reshape(-1) / first_gain.astype(F32)
    query_gain_sum = query_gain_sum.reshape(-1) / query_gain.astype(F32)
    second_gain_sum = second_gain_sum.reshape(-1) / second_gain.astype(F32)
    return (
        layer_out,
        input_grad,
        first_gain_sum,
        down_first,
        key_sum,
        value_sum,
        query_gain_sum,
        up_sum,
        out_sum,
        second_gain_sum,
        gate_sum,
        lift_sum,
        down_sum,
    )


def solution(mesh):
    fine = Mesh(mesh.devices.reshape(SIZES), AXES)
    split, groups = P(DP + SEQ, None), P(DP, None)
    matrix, vector = P(SEQ, None), P(SEQ)
    in_specs = (
        split,
        groups,
        vector,
        matrix,
        matrix,
        matrix,
        vector,
        matrix,
        matrix,
        vector,
        matrix,
        matrix,
        matrix,
        split,
    )
    out_specs = (
        split,
        split,
        vector,
        matrix,
        matrix,
        matrix,
        vector,
        matrix,
        matrix,
        vector,
        matrix,
        matrix,
        matrix,
    )
    return jax.shard_map(shards, mesh=fine, in_specs=in_specs, out_specs=out_specs, check_vma=False)
```

```python
import jax
import jax.numpy as jnp
from jax import lax
from jax.experimental import pallas as pl
from jax.experimental.pallas import tpu as pltpu
from jax.sharding import Mesh, PartitionSpec as P

NORM_EPSILON = 1e-05
F32 = jnp.float32
BF16 = jnp.bfloat16

AXES = ("v", "x", "y", "z", "c")
SIZES = (2, 4, 2, 4, 2)
DP, SEQ, ACROSS = ("v", "x"), ("y", "z", "c"), ("v", "x", "y")
SLOT = 384
KEY_CHUNK = 1024
BACK_CHUNK = 512


def turn(value, axis, step):
    size = SIZES[AXES.index(axis)]
    return lax.ppermute(value, axis, [(i, (i + step) % size) for i in range(size)])


def sibling(value):
    return turn(value, "c", 1)


def after(value, other):
    first = other[(0,) * other.ndim] if other.ndim else other
    return value + (first * 0).astype(value.dtype)


def rows(value, start, stop):
    return lax.slice_in_dim(value, start, stop, axis=0)


def exchange(parts, axes):
    return lax.all_to_all(parts, axes, 0, 0)


def spread(value, axes):
    count = 1
    for axis in axes:
        count *= SIZES[AXES.index(axis)]
    return exchange(jnp.broadcast_to(value[None], (count,) + value.shape), axes)


def total_of(parts):
    return jnp.sum(parts.astype(F32), axis=0)


def ring_gather(block, axis="z"):
    half = block.shape[0] // 2
    after_it, before_it = turn(block, axis, -1), turn(block, axis, 1)
    far_low = turn(rows(after_it, 0, half), axis, -1)
    far_high = turn(rows(before_it, half, 2 * half), axis, 1)
    return (block, far_low, far_high, after_it, before_it)


def ring_merge_kernel(part_ref, low_ref, high_ref, next_ref, back_ref):
    half = low_ref.shape[0]
    next_ref[half:, :] = part_ref[0, half:, :]
    next_ref[:half, :] = (part_ref[0, :half, :].astype(F32) + low_ref[...].astype(F32)).astype(BF16)
    back_ref[:half, :] = part_ref[1, :half, :]
    back_ref[half:, :] = (part_ref[1, half:, :].astype(F32) + high_ref[...].astype(F32)).astype(
        BF16
    )


def ring_scatter(parts, other=None):
    _, width, size = parts.shape
    half = width // 2
    got_low = turn(parts[1, :half], "z", 1)
    got_high = turn(parts[1, half:], "z", -1)
    if other is not None:
        got_low = after(got_low, other)
    half_spec = pl.BlockSpec((half, size), lambda i: (0, 0))
    full_spec = pl.BlockSpec((width, size), lambda i: (0, 0))
    to_next, to_back = pl.pallas_call(
        ring_merge_kernel,
        grid=(1,),
        out_shape=(jax.ShapeDtypeStruct((width, size), BF16),) * 2,
        in_specs=[pl.BlockSpec((2, width, size), lambda i: (1, 0, 0)), half_spec, half_spec],
        out_specs=(full_spec, full_spec),
        name="ring_merge",
    )(parts, got_low, got_high)
    return (
        parts[0].astype(F32)
        + turn(to_next, "z", 1).astype(F32)
        + turn(to_back, "z", -1).astype(F32)
    )


def inverse_rms(values):
    return lax.rsqrt(jnp.mean(values * values, axis=-1, keepdims=True) + NORM_EPSILON)


def rms_back(values, inv_root, gain_row, grad_normed):
    scaled = grad_normed * gain_row
    return inv_root * scaled - values * inv_root**3 * jnp.mean(
        scaled * values, axis=-1, keepdims=True
    )


def layout(lengths, token_index):
    doc_ends = jnp.cumsum(lengths)
    starts = doc_ends - lengths
    doc_id = jnp.sum((token_index[:, None] >= doc_ends[None, :]).astype(jnp.int32), axis=1)
    numbers = jnp.arange(lengths.shape[0], dtype=jnp.int32)
    doc_start = jnp.sum(jnp.where(doc_id[:, None] == numbers[None, :], starts[None, :], 0), axis=1)
    return doc_start


def rope_tables(position, head_width):
    half_width = head_width // 2
    frequency = 10000.0 ** (-(2.0 * jnp.arange(half_width, dtype=F32)) / head_width)
    angles = position.astype(F32)[:, None] * frequency[None, :]
    return (jnp.cos(angles), jnp.sin(angles))


def rotate(values, cosine, sine):
    half_width = cosine.shape[-1]
    low, high = values[..., :half_width], values[..., half_width:]
    return jnp.concatenate([low * cosine - high * sine, high * cosine + low * sine], axis=-1)


def rotate_back(grads, cosine, sine):
    return rotate(grads, cosine, -sine)


def dot(left, right):
    return jnp.dot(left, right, preferred_element_type=F32)


def dot_nt(left, right):
    return lax.dot_general(left, right, (((1,), (1,)), ((), ())), preferred_element_type=F32)


def dot_tn(left, right):
    return lax.dot_general(left, right, (((0,), (0,)), ((), ())), preferred_element_type=F32)


def masked(scores, first_key, place, begin):
    key = first_key + lax.broadcasted_iota(jnp.int32, scores.shape, 0)
    return jnp.where((key >= begin) & (key <= place), scores, -1e30)


def chunk_bounds(meta, block, width, size):
    number = meta[6 + block]
    count = ((number + 1) * width + size - 1) // size
    clear_from = jnp.minimum((meta[2 + block] + size - 1) // size, count)
    clear_to = jnp.maximum((number * width + 1) // size, clear_from)
    return clear_from, clear_to, count


def stack_lane(refs):
    return jnp.concatenate([ref[...] for ref in refs], axis=0)


def stack_heads(ref, block, head):
    count = ref.shape[2] // head
    return jnp.concatenate([ref[block, :, h * head : (h + 1) * head] for h in range(count)], axis=0)


def wide_row(ref, block, heads):
    return jnp.concatenate([ref[block]] * heads, axis=1)


def query_kernel(lane_a, lane_b, lane_c, lane_d, lane_e, up_ref, cos_ref, sin_ref, q_ref):
    blocks, width, size = q_ref.shape
    half = cos_ref.shape[1]
    head = 2 * half
    latent = stack_lane((lane_a, lane_b, lane_c, lane_d, lane_e))
    cosine, sine = cos_ref[...], sin_ref[...]
    for start in range(0, size, head):
        query = dot(latent, up_ref[:, start : start + head])
        low, high = query[:, :half], query[:, half:]
        turned = ((low * cosine - high * sine), (high * cosine + low * sine))
        for part, value in enumerate(turned):
            q_ref[:, :, start + part * half : start + (part + 1) * half] = (
                (value * head**-0.5).astype(BF16).reshape(blocks, width, half)
            )


def attend_kernel(meta, q_ref, kv_ref, place_ref, begin_ref, out_ref, log_ref):
    blocks, width, size = q_ref.shape
    head = kv_ref.shape[1] // 2
    heads = size // head
    rows_all = heads * width

    @pl.loop(0, blocks)
    def per_block(block):
        clear_from, clear_to, count = chunk_bounds(meta, block, width, KEY_CHUNK)
        place, begin = wide_row(place_ref, block, heads), wide_row(begin_ref, block, heads)
        query = stack_heads(q_ref, block, head)

        def chunk(step, carry, clear):
            top, total, mixed = carry
            start = pl.multiple_of(step * KEY_CHUNK, KEY_CHUNK)
            scores = dot_nt(kv_ref[pl.ds(start, KEY_CHUNK), :head], query)
            if not clear:
                scores = masked(scores, start, place, begin)
            new_top = jnp.maximum(top, jnp.max(scores, axis=0, keepdims=True))
            factor = jnp.exp(top - new_top)
            weights = jnp.exp(scores - new_top)
            total = total * factor + jnp.sum(weights, axis=0, keepdims=True)
            mixed = mixed * factor + dot_tn(
                kv_ref[pl.ds(start, KEY_CHUNK), head:], weights.astype(BF16)
            )
            return (new_top, total, mixed)

        carry = (
            jnp.full((1, rows_all), -1e30, F32),
            jnp.zeros((1, rows_all), F32),
            jnp.zeros((head, rows_all), F32),
        )
        carry = lax.fori_loop(0, clear_from, lambda s, w: chunk(s, w, False), carry)
        carry = lax.fori_loop(clear_from, clear_to, lambda s, w: chunk(s, w, True), carry)
        carry = lax.fori_loop(clear_to, count, lambda s, w: chunk(s, w, False), carry)
        top, total, mixed = carry
        result = (mixed / total).T.astype(BF16)
        for h in range(heads):
            out_ref[block, :, h * head : (h + 1) * head] = result[h * width : (h + 1) * width]
        log_ref[block] = top + jnp.log(total)


def attend_back_kernel(
    meta,
    branch_a,
    branch_b,
    branch_c,
    branch_d,
    branch_e,
    kv_ref,
    up_ref,
    proj_a,
    proj_b,
    proj_c,
    proj_d,
    cos_ref,
    sin_ref,
    place_ref,
    begin_ref,
    q_ref,
    out_ref,
    log_ref,
    lane_a,
    lane_b,
    lane_c,
    lane_d,
    lane_e,
    gq_ref,
    latent_ref,
    kv_own,
    kv_sib,
    out_own,
    out_sib,
    up_own,
    up_sib,
    grads,
    key_grad,
    value_grad,
):
    blocks, width, _ = q_ref.shape
    head = kv_ref.shape[1] // 2
    half = head // 2
    heads = q_ref.shape[2] // head
    branch = stack_lane((branch_a, branch_b, branch_c, branch_d, branch_e))
    y = meta[0]
    for at, (ref, yy) in enumerate(
        ((proj_a, y), (proj_b, 1 - y), (proj_c, y), (proj_d, 1 - y))
    ):
        first = pl.multiple_of((at // 2 * 2 + yy) * head, head)
        value = dot_nt(branch, ref[...])
        grads[:, :, pl.ds(first, head)] = value.astype(BF16).reshape(blocks, width, head)
    key_grad[...] = jnp.zeros_like(key_grad)
    value_grad[...] = jnp.zeros_like(value_grad)


    @pl.loop(0, blocks)
    def per_block(block):
        clear_from, clear_to, count = chunk_bounds(meta, block, width, BACK_CHUNK)
        place, begin = wide_row(place_ref, block, heads), wide_row(begin_ref, block, heads)
        token = pl.ds(pl.multiple_of(block * width, width), width)
        cosine, sine = cos_ref[token, :], sin_ref[token, :]
        query, grad, out = (stack_heads(ref, block, head) for ref in (q_ref, grads, out_ref))
        row_dot = jnp.sum((grad.astype(F32) * out.astype(F32)).T, axis=0, keepdims=True)
        log_total = log_ref[block]

        def chunk(step, acc, clear):
            start = pl.multiple_of(step * BACK_CHUNK, BACK_CHUNK)
            span = pl.ds(start, BACK_CHUNK)
            key_chunk = kv_ref[span, :head]
            scores = dot_nt(key_chunk, query)
            if not clear:
                scores = masked(scores, start, place, begin)
            probs = jnp.exp(scores - log_total)
            grad_probs = dot_nt(kv_ref[span, head:], grad)
            grad_scores = (probs * (grad_probs - row_dot)).astype(BF16)
            value_grad[span, :] += dot(probs.astype(BF16), grad)
            key_grad[span, :] += dot(grad_scores, query)
            return acc + dot_tn(grad_scores, key_chunk)

        acc = jnp.zeros((heads * width, head), F32)
        acc = lax.fori_loop(0, clear_from, lambda s, w: chunk(s, w, False), acc)
        acc = lax.fori_loop(clear_from, clear_to, lambda s, w: chunk(s, w, True), acc)
        acc = lax.fori_loop(clear_to, count, lambda s, w: chunk(s, w, False), acc)
        acc = acc * (head**-0.5)
        for h in range(heads):
            value = acc[h * width : (h + 1) * width]
            low, high = value[:, :half], value[:, half:]
            start = h * head
            gq_ref[block, :, start : start + half] = (low * cosine + high * sine).astype(BF16)
            gq_ref[block, :, start + half : start + head] = (high * cosine - low * sine).astype(BF16)

    grad_query = gq_ref[...].reshape(blocks * width, heads * head)
    size = latent_ref.shape[2]
    piece = 256
    for start in range(0, size, piece):
        value = dot_nt(grad_query, up_ref[start : start + piece, :])
        for slot in range(blocks):
            block = value[slot * width : (slot + 1) * width].astype(BF16)
            latent_ref[(meta[6 + slot] // 2) % 4, :, start : start + piece] = block
    mixed = out_ref[...].reshape(blocks * width, heads * head)
    latent = stack_lane((lane_a, lane_b, lane_c, lane_d, lane_e))
    for h in range(heads):
        span = slice(h * head, (h + 1) * head)
        at = slice((h % 2) * head, (h % 2 + 1) * head)
        target = (out_own, out_sib)[h // 2]
        target[at, :] = dot_tn(mixed[:, span], branch).astype(BF16)
        target = (up_own, up_sib)[h // 2]
        target[:, at] = dot_tn(latent, grad_query[:, span]).astype(BF16)
    c = meta[1]
    for chip in range(2 * blocks):
        for target, cc in ((kv_own, c), (kv_sib, 1 - c)):
            span = pl.ds(pl.multiple_of((chip * 2 + cc) * width, width), width)
            target[chip, :, :head] = key_grad[span, :].astype(BF16)
            target[chip, :, head:] = value_grad[span, :].astype(BF16)


def kernel_specs(count):
    smem = pl.BlockSpec(memory_space=pltpu.SMEM)
    vmem = pl.BlockSpec(memory_space=pltpu.VMEM)
    return [smem] + [vmem] * count


def column_kernel(meta, normed_ref, *targets):
    width = targets[0].shape[0]
    z, c = meta[0], meta[1]
    for step, target in zip((0, 2, 1, 3), targets):
        place = (z + 4 - step) % 4
        for at, (cc, y) in enumerate(((c, 0), (c, 1), (1 - c, 0), (1 - c, 1))):
            start = pl.multiple_of(((y * 4 + place) * 2 + cc) * width, width)
            target[:, at * width : (at + 1) * width] = normed_ref[:, pl.ds(start, width)]


def first_kernel(col_a, col_b, col_c, col_d, g_a, g_b, g_c, g_d, g_e, own_ref, other_ref):
    columns = stack_lane((col_a, col_b, col_c, col_d))
    grads = stack_lane((g_a, g_b, g_c, g_d, g_e))
    half = own_ref.shape[0]
    own_ref[...] = dot_tn(columns[:, :half], grads)
    other_ref[...] = dot_tn(columns[:, half:], grads).astype(BF16)


def first_weights(columns, lane):
    half, size = columns[0].shape[1] // 2, lane[0].shape[1]
    return pl.pallas_call(
        first_kernel,
        out_shape=(
            jax.ShapeDtypeStruct((half, size), F32),
            jax.ShapeDtypeStruct((half, size), BF16),
        ),
        in_specs=kernel_specs(9)[1:],
        out_specs=tuple(kernel_specs(2)[1:]),
        compiler_params=pltpu.CompilerParams(vmem_limit_bytes=16 * 2**20),
        cost_estimate=pl.CostEstimate(
            flops=800_000_000, bytes_accessed=5_000_000, transcendentals=0
        ),
        name="first_weights",
    )(*columns, *lane)


def pick_columns(normed, z, c):
    width = normed.shape[0]
    return pl.pallas_call(
        column_kernel,
        out_shape=(jax.ShapeDtypeStruct((width, 4 * width), BF16),) * 4,
        in_specs=kernel_specs(1),
        out_specs=tuple(kernel_specs(4)[1:]),
        name="pick_columns",
    )(jnp.stack([z, c]).astype(jnp.int32), normed)


def make_queries(lane, up, cosine, sine, blocks):
    width = lane[0].shape[0]
    return pl.pallas_call(
        query_kernel,
        out_shape=jax.ShapeDtypeStruct((blocks, width, up.shape[1]), BF16),
        in_specs=kernel_specs(8)[1:],
        out_specs=kernel_specs(1)[1],
        compiler_params=pltpu.CompilerParams(vmem_limit_bytes=24 * 2**20),
        cost_estimate=pl.CostEstimate(
            flops=1_100_000_000, bytes_accessed=5_000_000, transcendentals=0
        ),
        name="make_queries",
    )(*lane, up, cosine, sine)


def attend(meta, query, kv, place, begin):
    blocks, width, size = query.shape
    head = kv.shape[1] // 2
    shape = jax.ShapeDtypeStruct
    return pl.pallas_call(
        attend_kernel,
        out_shape=(
            shape(query.shape, BF16),
            shape((blocks, 1, size // head * width), F32),
        ),
        in_specs=kernel_specs(4),
        out_specs=tuple(kernel_specs(2)[1:]),
        compiler_params=pltpu.CompilerParams(vmem_limit_bytes=32 * 2**20),
        cost_estimate=pl.CostEstimate(
            flops=20_000_000_000, bytes_accessed=5_000_000, transcendentals=3_400_000
        ),
        name="attend",
    )(meta, query, kv, place, begin)


def project_kernel(meta, mixed_ref, own_ref, across_ref, sib_ref, across_sib_ref, part_ref):
    blocks, width, model = part_ref.shape
    head = own_ref.shape[0]
    y = meta[0]
    piece = 512
    for start in range(0, model, piece):
        total = None
        for at, (ref, yy) in enumerate(
            ((own_ref, y), (across_ref, 1 - y), (sib_ref, y), (across_sib_ref, 1 - y))
        ):
            first = pl.multiple_of((at // 2 * 2 + yy) * head, head)
            left = mixed_ref[:, :, pl.ds(first, head)].reshape(blocks * width, head)
            value = dot(left, ref[:, start : start + piece])
            total = value if total is None else total + value
        part_ref[:, :, start : start + piece] = total.astype(BF16).reshape(blocks, width, piece)


def project(meta, mixed, pieces):
    blocks, width, _ = mixed.shape
    model = pieces[0].shape[1]
    return pl.pallas_call(
        project_kernel,
        out_shape=jax.ShapeDtypeStruct((blocks, width, model), BF16),
        in_specs=kernel_specs(5),
        out_specs=kernel_specs(1)[1],
        compiler_params=pltpu.CompilerParams(vmem_limit_bytes=24 * 2**20),
        cost_estimate=pl.CostEstimate(
            flops=2_200_000_000, bytes_accessed=7_500_000, transcendentals=0
        ),
        name="project",
    )(meta, mixed, *pieces)


def feed_kernel(n_ref, cot_ref, own_ref, sib_ref, down_ref, hid_ref, go_ref, gs_ref, back_ref):
    slot = down_ref.shape[0] // 2
    blocks, _, size = own_ref.shape
    normed = n_ref[...]
    grad_hidden = dot_nt(cot_ref[...], down_ref[...])
    back = None
    for at, (weight, grad_ref) in enumerate(((own_ref, go_ref), (sib_ref, gs_ref))):
        span = slice(at * slot, (at + 1) * slot)
        both = jnp.concatenate([dot(normed, weight[i]) for i in range(blocks)], axis=1)
        gate, lift = both[:, :slot], both[:, slot:]
        grad = grad_hidden[:, span]
        sigmoid = jax.nn.sigmoid(gate)
        active = gate * sigmoid
        hid_ref[:, span] = (active * lift).astype(BF16)
        grad_ref[:, :slot] = (grad * lift * sigmoid * (1.0 + gate * (1.0 - sigmoid))).astype(BF16)
        grad_ref[:, slot:] = (grad * active).astype(BF16)
        for i in range(blocks):
            part = dot_nt(grad_ref[:, i * size : (i + 1) * size], weight[i])
            back = part if back is None else back + part
    back_ref[...] = back.astype(BF16)


def combine_kernel(feed_ref, feed_got, down_ref, down_got, out_ref):
    parts, owners, quarter, _ = out_ref.shape
    wide = feed_ref.shape[1]
    for owner in range(owners):
        for x in range(parts):
            span = slice((owner * parts + x) * quarter, (owner * parts + x + 1) * quarter)
            feed = feed_ref[span, :].astype(F32) + feed_got[span, :].astype(F32)
            down = down_ref[span, :].astype(F32) + down_got[span, :].astype(F32)
            out_ref[x, owner, :, :wide] = feed.astype(BF16)
            out_ref[x, owner, :, wide:] = down.astype(BF16)


def combine(feed, feed_got, down, down_got):
    model, wide = feed.shape
    parts, owners, steps = 4, 16, 4
    share = model // (parts * owners)
    total = wide + down.shape[1]

    def row(value):
        return pl.BlockSpec((model // steps, value.shape[1]), lambda i: (i, 0))

    result = pl.pallas_call(
        combine_kernel,
        out_shape=jax.ShapeDtypeStruct((parts, owners, share, total), BF16),
        grid=(steps,),
        in_specs=[row(feed), row(feed_got), row(down), row(down_got)],
        out_specs=pl.BlockSpec((parts, owners // steps, share, total), lambda i: (0, i, 0, 0)),
        compiler_params=pltpu.CompilerParams(vmem_limit_bytes=24 * 2**20),
        cost_estimate=pl.CostEstimate(flops=5_000_000, bytes_accessed=15_000_000, transcendentals=0),
        name="combine",
    )(feed, feed_got, down, down_got)
    return result.reshape(model, total)


def spill_kernel(sum_ref, gate_weight, lift_weight, gate_ref, lift_ref, down_ref, gain_ref):
    parts, owners, quarter, _ = sum_ref.shape
    hidden = down_ref.shape[0]
    width = parts * quarter
    for owner in range(owners):
        for x in range(parts):
            span = slice(x * quarter, (x + 1) * quarter)
            at = slice(owner * hidden, (owner + 1) * hidden)
            gate_ref[span, at] = sum_ref[x, owner, :, :hidden].astype(F32)
            lift_ref[span, at] = sum_ref[x, owner, :, SLOT : SLOT + hidden].astype(F32)
        block = sum_ref[:, owner, :, 2 * SLOT :].astype(F32).reshape(width, SLOT)
        down_ref[:, owner * width : (owner + 1) * width] = block.T[:hidden]
    gain_ref[...] = jnp.sum(
        gate_ref[...] * gate_weight[...].astype(F32) + lift_ref[...] * lift_weight[...].astype(F32),
        axis=1,
        keepdims=True,
    )


def spill(summed, gate_weight, lift_weight, hidden):
    parts, owners, quarter, _ = summed.shape
    shape = jax.ShapeDtypeStruct
    return pl.pallas_call(
        spill_kernel,
        out_shape=(shape((parts * quarter, owners * hidden), F32),) * 2
        + (shape((hidden, owners * parts * quarter), F32), shape((parts * quarter, 1), F32)),
        in_specs=kernel_specs(3)[1:],
        out_specs=tuple(kernel_specs(4)[1:]),
        compiler_params=pltpu.CompilerParams(vmem_limit_bytes=40 * 2**20),
        cost_estimate=pl.CostEstimate(flops=5_000_000, bytes_accessed=17_000_000, transcendentals=0),
        name="spill",
    )(summed, gate_weight, lift_weight)


def heads_kernel(fence, out_ref, out_got, up_ref, up_got, pack_ref):
    model = out_ref.shape[1]
    head = out_ref.shape[0] // 2
    share = head // 8
    owners = 16
    depth = up_ref.shape[0] // owners
    few = depth // 8
    for y in range(2):
        for part in range(8):
            at = part * 2 + y
            span = slice(y * head + part * share, y * head + (part + 1) * share)
            total = out_ref[span, :].astype(F32) + out_got[span, :].astype(F32)
            pack_ref[at, :share, :] = total.astype(BF16)
            cols = slice(y * head, (y + 1) * head)
            for pair in range(owners // 2):
                slabs = []
                for owner in (2 * pair, 2 * pair + 1):
                    rows_at = slice(owner * depth + part * few, owner * depth + (part + 1) * few)
                    slabs.append(
                        up_ref[rows_at, cols].astype(F32) + up_got[rows_at, cols].astype(F32)
                    )
                pack_ref[at, share:, pair * head : (pair + 1) * head] = jnp.concatenate(
                    slabs, axis=0
                ).astype(BF16)


def pack_heads(fence, out, out_got, up, up_got):
    head, model = out.shape[0] // 2, out.shape[1]
    return pl.pallas_call(
        heads_kernel,
        out_shape=jax.ShapeDtypeStruct((16, head // 8 + 16, model), BF16),
        in_specs=kernel_specs(4),
        out_specs=kernel_specs(1)[1],
        compiler_params=pltpu.CompilerParams(vmem_limit_bytes=24 * 2**20),
        cost_estimate=pl.CostEstimate(flops=2_000_000, bytes_accessed=9_500_000, transcendentals=0),
        name="pack_heads",
    )(fence, out, out_got, up, up_got)


def finish_kernel(
    last_ref,
    down_weight,
    key_weight,
    value_weight,
    up_weight,
    out_ref,
    up_ref,
    down_ref,
    key_ref,
    value_ref,
    first_ref,
    query_ref,
):
    parts, _, model = last_ref.shape
    out_rows, up_rows = out_ref.shape[0] // parts, up_ref.shape[0] // parts
    rows_each = down_ref.shape[0] // parts
    latent, head = down_ref.shape[1], key_ref.shape[1]
    for part in range(parts):
        out_ref[part * out_rows : (part + 1) * out_rows, :] = last_ref[part, :out_rows, :].astype(
            F32
        )
        up = last_ref[part, out_rows : out_rows + 2 * up_rows, :].astype(F32)
        span = slice(part * up_rows, (part + 1) * up_rows)
        up_ref[span, :model] = up[:up_rows]
        up_ref[span, model:] = up[up_rows:]
        first = last_ref[part, out_rows + 2 * up_rows :, :].astype(F32)
        span = slice(part * rows_each, (part + 1) * rows_each)
        down_ref[span, :] = first[:, :latent]
        key_ref[span, :] = first[:, latent : latent + head]
        value_ref[span, :] = first[:, latent + head : latent + 2 * head]
    total = None
    for grad, weight in ((down_ref, down_weight), (key_ref, key_weight), (value_ref, value_weight)):
        value = jnp.sum(grad[...] * weight[...].astype(F32), axis=1, keepdims=True)
        total = value if total is None else total + value
    first_ref[...] = total
    query_ref[...] = jnp.sum(up_ref[...] * up_weight[...].astype(F32), axis=1, keepdims=True)


def finish(last, down_weight, key_weight, value_weight, up_weight):
    parts, _, model = last.shape
    shape = jax.ShapeDtypeStruct
    width, depth, head = down_weight.shape[0], up_weight.shape[0], key_weight.shape[1]
    return pl.pallas_call(
        finish_kernel,
        out_shape=(
            shape((head, model), F32),
            shape(up_weight.shape, F32),
            shape(down_weight.shape, F32),
            shape(key_weight.shape, F32),
            shape(value_weight.shape, F32),
            shape((width, 1), F32),
            shape((depth, 1), F32),
        ),
        in_specs=kernel_specs(5)[1:],
        out_specs=tuple(kernel_specs(7)[1:]),
        compiler_params=pltpu.CompilerParams(vmem_limit_bytes=24 * 2**20),
        cost_estimate=pl.CostEstimate(flops=2_000_000, bytes_accessed=8_000_000, transcendentals=0),
        name="finish",
    )(last, down_weight, key_weight, value_weight, up_weight)


def feed_forward(normed, cotangent, own, sib, down):
    count, model = normed.shape
    tile, slots = 256, down.shape[0]
    row = pl.BlockSpec((tile, model), lambda i: (i, 0))
    slot_row = pl.BlockSpec((tile, slots), lambda i: (i, 0))

    def fixed(value):
        return pl.BlockSpec(value.shape, lambda i: (0,) * value.ndim)

    shape = jax.ShapeDtypeStruct
    return pl.pallas_call(
        feed_kernel,
        grid=(count // tile,),
        out_shape=(shape((count, slots), BF16),) * 3 + (shape((count, model), BF16),),
        in_specs=[row, row, fixed(own), fixed(sib), fixed(down)],
        out_specs=(slot_row,) * 3 + (row,),
        compiler_params=pltpu.CompilerParams(vmem_limit_bytes=52 * 2**20),
        cost_estimate=pl.CostEstimate(
            flops=19_000_000_000, bytes_accessed=32_000_000, transcendentals=800_000
        ),
        name="feed_forward",
    )(normed, cotangent, own, sib, down)


def attend_back(meta, branch, kv, up, proj, cosine, sine, place, begin, query, out, log, lane):
    blocks, _, width = place.shape
    head = kv.shape[1] // 2
    shape = jax.ShapeDtypeStruct
    return pl.pallas_call(
        attend_back_kernel,
        out_shape=(
            shape(query.shape, BF16),
            shape((blocks, width, up.shape[0]), BF16),
            shape((2 * blocks, width, 2 * head), BF16),
            shape((2 * blocks, width, 2 * head), BF16),
            shape((2 * head, proj[0].shape[1]), BF16),
            shape((2 * head, proj[0].shape[1]), BF16),
            shape((up.shape[0], 2 * head), BF16),
            shape((up.shape[0], 2 * head), BF16),
        ),
        in_specs=kernel_specs(23),
        out_specs=tuple(kernel_specs(8)[1:]),
        scratch_shapes=[pltpu.VMEM(query.shape, BF16)]
        + [pltpu.VMEM((kv.shape[0], head), F32)] * 2,
        compiler_params=pltpu.CompilerParams(vmem_limit_bytes=48 * 2**20),
        cost_estimate=pl.CostEstimate(
            flops=24_000_000_000, bytes_accessed=20_000_000, transcendentals=3_400_000
        ),
        name="attend_back",
    )(meta, *branch, kv, up, *proj, cosine, sine, place, begin, query, out, log, *lane)


def shards(
    tokens,
    doc_lengths,
    first_gain,
    query_down,
    key_proj,
    value_proj,
    query_gain,
    query_up,
    out_proj,
    second_gain,
    gate_proj,
    up_proj,
    down_proj,
    cotangent,
):
    width, model = tokens.shape
    latent_width = query_down.shape[1]
    head = key_proj.shape[1]
    depth = query_up.shape[0]
    hidden_width = gate_proj.shape[1] // 16
    lane_width = latent_width + 2 * head

    v, x, y, z, c = (lax.axis_index(axis) for axis in AXES)

    weights = lax.all_gather(
        jnp.concatenate([query_down, key_proj, value_proj], axis=1), SEQ, axis=0, tiled=True
    )

    gain_rows = jnp.zeros((16, head), BF16)
    gain_rows = gain_rows.at[0, :width].set(first_gain).at[1, :width].set(second_gain)
    gain_rows = gain_rows.at[2, :depth].set(query_gain)
    heads = query_up.reshape(depth, 2, 8, head)
    quarter = width // 4
    feed_rows = [
        jnp.pad(
            lax.dynamic_slice_in_dim(weight, x * quarter, quarter, 0).reshape(
                quarter, 16, hidden_width
            ),
            ((0, 0), (0, 0), (0, SLOT - hidden_width)),
        )
        for weight in (gate_proj, up_proj)
    ]
    feed_rows = jnp.concatenate(feed_rows, axis=2)
    parts = [
        jnp.broadcast_to(heads[:, at].transpose(1, 0, 2)[None], (2, 8, depth, head)).reshape(
            16, depth, head
        )
        for at in range(2)
    ]
    parts = parts + [
        feed_rows[..., at * head : (at + 1) * head].transpose(1, 0, 2) for at in range(3)
    ]
    parts = parts + [jnp.broadcast_to(gain_rows[None], (16, 16, head))]
    swapped_weights = exchange(jnp.concatenate(parts, axis=1), SEQ)
    first_row = 2 * depth + 3 * quarter
    gain_one = swapped_weights[:, first_row, :width].reshape(1, model).astype(F32)
    gain_two = swapped_weights[:, first_row + 1, :width].reshape(1, model).astype(F32)
    gain_query = swapped_weights[:, first_row + 2, :depth].reshape(1, latent_width).astype(F32)
    up_pair = jnp.concatenate(
        [
            swapped_weights[:, at * depth : (at + 1) * depth].reshape(latent_width, head)
            for at in range(2)
        ],
        axis=1,
    )
    up_chip = jnp.concatenate([up_pair, sibling(up_pair)], axis=1)
    feed_parts = swapped_weights[:, 2 * depth : first_row].reshape(16 * 3 * quarter, head)

    lengths = doc_lengths[0]
    z_at = jnp.stack([z, (z + 2) % 4, (z + 1) % 4, (z + 3) % 4])
    blocks = (y * 4 + z_at) * 2 + c
    token_index = blocks[:, None] * width + jnp.arange(width, dtype=jnp.int32)[None, :]
    doc_start = layout(lengths, token_index.reshape(-1)).reshape(token_index.shape)
    cosine, sine = rope_tables((token_index - doc_start).reshape(-1), head)
    meta = jnp.concatenate([jnp.stack([y, c]), jnp.max(doc_start, axis=1), blocks])
    meta = meta.astype(jnp.int32)
    place_row = token_index[:, None, :]
    begin_row = doc_start[:, None, :]
    cos_own, sin_own = cosine[:width], sine[:width]

    tokens_float = tokens.astype(F32)
    inv_one = inverse_rms(tokens_float)
    with jax.named_scope("out_chip"):
        out_sib = sibling(out_proj)
    for piece in (up_chip, out_sib):
        gain_one = after(gain_one, piece)
    normed = (tokens_float * inv_one * gain_one).astype(BF16)
    first = dot(normed, weights)
    latent = first[:, :latent_width]
    inv_latent = inverse_rms(latent)
    latent_n = (latent * inv_latent * gain_query).astype(BF16)
    key_rot = rotate(first[:, latent_width : latent_width + head], cos_own, sin_own).astype(BF16)
    value_low = first[:, latent_width + head :].astype(BF16)

    kv = lax.all_gather(
        jnp.concatenate([key_rot, value_low], axis=1), SEQ, axis=0, tiled=True
    )
    with jax.named_scope("lane"):
        lane = ring_gather(latent_n)
    with jax.named_scope("out_chip"):
        out_across = turn(after(out_proj, first), "y", 1)
    lane = (lane[0], after(lane[1], out_across)) + lane[2:]
    query_rot = make_queries(lane, up_chip, cosine, sine, 4)
    with jax.named_scope("out_chip"):
        out_across_sib = sibling(after(out_across, query_rot))
    attended, log_total = attend(meta, query_rot, kv, place_row, begin_row)
    out_pieces = (out_proj, out_across, out_sib, out_across_sib)
    cot_all = lax.all_gather(after(cotangent, first), ("y", "z"), axis=0, tiled=True)
    attended_rows = attended.reshape(4 * width, 4 * head)
    mixed = project(meta, attended, out_pieces)
    with jax.named_scope("residual"):
        residual = tokens_float + ring_scatter(mixed)
    inv_two = inverse_rms(residual)
    normed_two = (residual * inv_two * gain_two).astype(BF16)

    normed_all = lax.all_gather(normed_two, ("y", "z"), axis=0, tiled=True)
    with jax.named_scope("feed_weights"):
        feed_ring = ring_gather(after(feed_parts, normed_two), "x")
        feed_own = jnp.zeros((3, 16, 4, quarter, head), BF16)
        for part, step, first_owner in zip(feed_ring, (0, 2, 2, 1, 3), (0, 0, 8, 0, 0)):
            part = part.reshape(-1, 3, quarter, head).transpose(1, 0, 2, 3)[:, :, None]
            feed_own = lax.dynamic_update_slice(
                feed_own, part, (0, first_owner, (x + step) % 4, 0, 0)
            )
        feed_own = feed_own.reshape(3, model, head)
        feed_sib = sibling(feed_own)
        down_own = jnp.pad(down_proj, ((0, SLOT - hidden_width), (0, 0)))
        down_chip = jnp.concatenate([down_own, sibling(after(down_own, kv))], axis=0)
    hidden, grad_own, grad_sib, back = feed_forward(
        normed_all, cot_all, feed_own, feed_sib, down_chip
    )
    grad_normed_two = lax.psum_scatter(back, ("y", "z"), scatter_dimension=0, tiled=True)
    grad_normed_two = grad_normed_two.astype(F32)

    with jax.named_scope("feed_grad"):
        feed_other = sibling(dot_tn(normed_all, grad_sib).astype(BF16))
        down_other = sibling(dot_tn(cot_all, hidden[:, SLOT:]).astype(BF16))
        feed_grad = dot_tn(normed_all, grad_own).astype(BF16)
        down_grad = dot_tn(cot_all, hidden[:, :SLOT]).astype(BF16)
    with jax.named_scope("feed_grad"):
        feed_grad = combine(feed_grad, feed_other, down_grad, down_other)
        feed_part = lax.psum_scatter(feed_grad, "x", scatter_dimension=0, tiled=True)
        fed = lax.optimization_barrier(dot(hidden, down_chip).astype(BF16))
    grad_normed_two = after(after(grad_normed_two, feed_grad), fed)
    grad_two = rms_back(residual, inv_two, gain_two, grad_normed_two)
    grad_residual = cotangent.astype(F32) + grad_two

    with jax.named_scope("branch"):
        branch = ring_gather(grad_residual.astype(BF16))
    with jax.named_scope("layer_out"):
        fed = fed.reshape(2, 4 * width, model)
        fed_own = lax.dynamic_index_in_dim(fed, y, 0, keepdims=False)
        fed_across = lax.dynamic_index_in_dim(fed, 1 - y, 0, keepdims=False)
        fed_across = turn(after(fed_across, grad_residual), "y", 1)
    grad_queries, latent_parts, kv_own, kv_sib, out_grad, out_grad_sib, up_grad, up_sib = attend_back(
        meta,
        branch,
        kv,
        up_chip,
        out_pieces,
        cosine,
        sine,
        place_row,
        begin_row,
        query_rot,
        attended,
        log_total,
        lane,
    )
    with jax.named_scope("kv_grad"):
        kv_grad = kv_own.astype(F32) + sibling(kv_sib).astype(F32)
        kv_grad = after(kv_grad, feed_part[0, 0] + fed_across[0, 0]).astype(BF16)
        kv_sum = total_of(exchange(kv_grad, ("y", "z")))
    with jax.named_scope("heads_grad"):
        heads_parts = pack_heads(
            (kv_sum[0, 0] * 0).astype(jnp.int32).reshape(1),
            out_grad,
            sibling(out_grad_sib),
            up_grad,
            sibling(up_sib),
        )
        heads_got = exchange(heads_parts, ACROSS)
    with jax.named_scope("layer_out"):
        fed = fed_own.astype(F32) + after(fed_across.astype(F32), heads_parts)
        fed_part = lax.psum_scatter(fed.astype(BF16), "z", scatter_dimension=0, tiled=True)
        layer_out = (residual + fed_part.astype(F32)).astype(BF16)
    with jax.named_scope("feed_grad"):
        feed_part = after(feed_part, kv_sum)
        feed_across = turn(feed_part, "v", 1)
        feed_part = (feed_part.astype(F32) + feed_across.astype(F32)).astype(BF16)
        feed_part = feed_part.reshape(16, quarter, 3 * SLOT)
        swapped = exchange(after(feed_part[..., : 2 * SLOT], heads_got), SEQ)
        feed_part = jnp.concatenate([swapped, feed_part[..., 2 * SLOT :]], axis=2)
        feed_sum = lax.all_gather(
            feed_part.reshape(16 * quarter, 3 * SLOT), "x", axis=0, tiled=True
        )
    with jax.named_scope("latent_grad"):
        latent_parts = latent_parts.reshape(4 * width, latent_width)
        grad_latent_n = lax.psum_scatter(latent_parts, "z", scatter_dimension=0, tiled=True)
        grad_latent_n = grad_latent_n.astype(F32)
    grad_keys = rotate_back(kv_sum[:, :head], cos_own, sin_own).astype(BF16)
    grad_values = kv_sum[:, head:].astype(BF16)
    grad_latent = rms_back(latent, inv_latent, gain_query, grad_latent_n)
    grad_latent = grad_latent.astype(BF16)
    grad_first = jnp.concatenate([grad_latent, grad_keys, grad_values], axis=1)
    with jax.named_scope("first_lane"):
        first_lane = ring_gather(grad_first)
    with jax.named_scope("columns"):
        columns = pick_columns(normed, z + (kv_sum[0, 0] * 0).astype(jnp.int32), c)
        columns = (columns[0],) + tuple(
            turn(part, "z", -step) for part, step in zip(columns[1:], (2, 1, 3))
        )
    own_first, first_other = first_weights(columns, first_lane)
    own_first = own_first + sibling(first_other).astype(F32)
    with jax.named_scope("heads_grad"):
        heads_part = total_of(heads_got).astype(BF16)
        out_part, up_part = heads_part[: head // 8], heads_part[head // 8 :]
        up_part = up_part.reshape(16, 8, head).transpose(1, 0, 2)
    grad_normed = dot_nt(grad_latent, weights[:, :latent_width])
    grad_normed = grad_normed + dot_nt(grad_first[:, latent_width:], weights[:, latent_width:])
    grad_one = rms_back(tokens_float, inv_one, gain_one, grad_normed)
    input_grad = grad_residual + grad_one

    share = width // 8
    tail = after(after(own_first, input_grad), swapped).reshape(2, 8, share, lane_width).transpose(1, 0, 2, 3)
    tail = total_of(exchange(tail.reshape(16, share, lane_width).astype(BF16), ACROSS))
    with jax.named_scope("up_grad"):
        up_part = exchange(after(up_part, tail).reshape(16, depth // 8, head), SEQ)
        up_part = up_part.reshape(2, 8, depth // 8, head).transpose(0, 2, 1, 3)
        up_part = up_part.reshape(-1, model)
    with jax.named_scope("heads_sum"):
        first_part = jnp.pad(tail.astype(BF16), ((0, 0), (0, model - lane_width)))
        last_sum = spread(jnp.concatenate([out_part, up_part, first_part], axis=0), DP)
    gate_sum, lift_sum, down_sum, second_gain_sum = spill(
        feed_sum.reshape(4, 16, quarter, 3 * SLOT), gate_proj, up_proj, hidden_width
    )
    out_sum, up_sum, down_first, key_sum, value_sum, first_gain_sum, query_gain_sum = finish(
        last_sum, query_down, after(key_proj, second_gain_sum), value_proj, query_up
    )
    first_gain_sum = first_gain_sum.reshape(-1) / first_gain.astype(F32)
    query_gain_sum = query_gain_sum.reshape(-1) / query_gain.astype(F32)
    second_gain_sum = second_gain_sum.reshape(-1) / second_gain.astype(F32)
    return (
        layer_out,
        input_grad,
        first_gain_sum,
        down_first,
        key_sum,
        value_sum,
        query_gain_sum,
        up_sum,
        out_sum,
        second_gain_sum,
        gate_sum,
        lift_sum,
        down_sum,
    )


def solution(mesh):
    fine = Mesh(mesh.devices.reshape(SIZES), AXES)
    split, groups = P(DP + SEQ, None), P(DP, None)
    matrix, vector = P(SEQ, None), P(SEQ)
    in_specs = (
        split,
        groups,
        vector,
        matrix,
        matrix,
        matrix,
        vector,
        matrix,
        matrix,
        vector,
        matrix,
        matrix,
        matrix,
        split,
    )
    out_specs = (
        split,
        split,
        vector,
        matrix,
        matrix,
        matrix,
        vector,
        matrix,
        matrix,
        vector,
        matrix,
        matrix,
        matrix,
    )
    return jax.shard_map(shards, mesh=fine, in_specs=in_specs, out_specs=out_specs, check_vma=False)
```
